32 devices in a mesh: dp: 8 (over y, x, core), blk: 4 (over z).
Axes of the slice: x: 2, y: 2, z: 4, core: 2. Of those that a mesh axis runs over, the one named last changes fastest.
Arguments:
- fields: float32 [8, 2048, 192], P('dp', 'blk'), may hold values from -6 to 6
- targets: float32 [8, 2048, 192], P('dp', 'blk'), may hold values from -6 to 6
- lead_time: float32 [8], P('dp'), may hold values from 0.25 to 3
- pixel_mask: int32 [8, 2048, 192], P('dp', 'blk'), may hold values from 0 to 1
- group_id: int32 [8], P('dp'), may hold values from 0 to 4, as said below
- slot_of: int32 [16], replicated, may hold values from 0 to 15, each once
- tiles: float32 [16, 1024, 1024], P('dp', 'blk'), may hold values from -0.1875 to 0.1875
- tiles_m: float32 [16, 1024, 1024], P('dp', 'blk'), may hold values from -7.6293945e-06 to 7.6293945e-06
- tiles_v: float32 [16, 1024, 1024], P('dp', 'blk'), may hold values from 1.214702e-12 to 4.858808e-12
- vectors: float32 [499, 1024], replicated
- vec_m: float32 [499, 1024], replicated, may hold values from -3.0517578e-05 to 3.0517578e-05
- vec_v: float32 [499, 1024], replicated, may hold values from 1.9666602e-11 to 7.7509554e-11
Outputs:
- loss: float32 [], replicated
- grad_norm: float32 [], replicated
- tiles_new: float32 [16, 1024, 1024], P('dp', 'blk')
- tiles_m_new: float32 [16, 1024, 1024], P('dp', 'blk')
- tiles_v_new: float32 [16, 1024, 1024], P('dp', 'blk')
- vectors_new: float32 [499, 1024], replicated
- vec_m_new: float32 [499, 1024], replicated
- vec_v_new: float32 [499, 1024], replicated
The draws below stay inside these ranges and needn't reach their ends.
Inputs may be any that keep to these rules, and one draw needn't show every extreme that they name: `group_id`: every one of the 5 sources has at least one sample. `slot_of`: each slot number once.
All inputs are finite; a program needn't handle non-finite values.
Results may differ from the reference program's by a relative error of at most 0.0055.
Values may be sent and summed in bfloat16 or wider, within the bound.
No kernel may reach another device: no remote copies, remote signals or barrier semaphores. Data moves between devices by JAX's collectives and lax.ppermute only.
A program may use at most 832 MiB of HBM per device.

```python
import math
import jax
import jax.numpy as jnp
from jax import lax

D = 1024
HEADS = 16
HD = 64
FF = 4096
VARS = 48
PIX = 4
PROWS = 32
PCOLS = 64
PATCHES = 2048
GROUPS = 5
SAMPLES = 8
TILES = 16
NVEC = 499
STEP = 10


def draw_pixel_mask(key, part):
    draws = jax.random.randint(key, (SAMPLES, PATCHES, VARS * PIX), 0, 1000)
    patch = jnp.arange(PATCHES)[None, :, None]
    sample = jnp.arange(SAMPLES)[:, None, None]
    limit = (250 + 500 * patch // PATCHES) * (100 + 200 * sample // SAMPLES) // 300
    return (draws < limit).astype(jnp.int32)


def draw_group_id(key, part):
    keys = jax.random.split(key, 3)
    table = jnp.array([0, 0, 0, 0, 0, 0, 1, 1, 1, 1, 2, 2, 2, 3, 4], dtype=jnp.int32)
    picks = jax.random.randint(keys[0], (SAMPLES,), 0, 15)
    labels = jax.random.permutation(keys[1], GROUPS)
    first = jax.random.permutation(keys[2], GROUPS)
    index = jnp.arange(SAMPLES)
    common = labels[table[picks]]
    return jnp.where(index < GROUPS, first[jnp.minimum(index, GROUPS - 1)], common).astype(jnp.int32)


def draw_vectors(key, part):
    noise = jax.random.normal(key, (NVEC, D), jnp.float32)
    ramp_low, ramp_span = (0.6, 1.2)
    row_index = jnp.arange(NVEC)[:, None]
    column = jnp.arange(D)[None, :].astype(jnp.float32) / D
    extra_start = VARS * (2 * PIX + 2)
    relative = row_index - extra_start
    scales = jnp.where(row_index < VARS * PIX, 0.5, 0.2)
    scales = jnp.where((row_index >= VARS * (PIX + 2)) & (row_index < extra_start), D ** (-0.5), scales)
    scales = jnp.where(relative == 0, 1.0, scales)
    scales = jnp.where(relative == 1, 0.5, scales)
    values = noise * scales
    is_gain = (relative == 6) | (relative == 10) | (relative == 13)
    gains = (ramp_low + ramp_span * column) * (1.0 + 0.1 * noise)
    return jnp.where(is_gain, gains, values).astype(jnp.float32)


def level_of(key, shape, cuts, low, top_value):
    def one(position, blocks):
        steps = jax.random.uniform(jax.random.fold_in(jax.random.fold_in(key, 6), position), (blocks,), jnp.float32, low / len(cuts), top_value / len(cuts))
        return jnp.repeat(jnp.exp(steps), shape[position] // blocks).reshape((-1,) + (1,) * (len(shape) - position - 1))

    level = one(*cuts[0])
    for cut in cuts[1:]:
        level = level * one(*cut)
    return level


def centred(own_key, shape, scale, most, shards=(), kind=jnp.bfloat16):
    values = jax.random.normal(own_key, shape, jnp.float32) * scale
    if len(shards) > 0:
        values = level_of(own_key, shape, shards, -0.22, 0.18) * values
    return jnp.clip(values, min=-most, max=most).astype(kind)


def setup_inputs(seed: int = 0) -> dict:
    seeds = jax.random.split(jax.random.key(seed), 13)
    return {
        "fields": centred(seeds[0], (SAMPLES, PATCHES, VARS * PIX), 1.0, 6.0, ((0, 8), (1, 4)), jnp.float32),
        "targets": centred(seeds[1], (SAMPLES, PATCHES, VARS * PIX), 1.0, 6.0, ((0, 8), (1, 4)), jnp.float32),
        "lead_time": jnp.clip(0.25 + 2.75 * jax.random.uniform(seeds[2], (SAMPLES,), jnp.float32) ** level_of(seeds[2], (SAMPLES,), ((0, 8),), -0.2, 0.2), 0.25, 3.0),
        "pixel_mask": draw_pixel_mask(jax.random.fold_in(seeds[12], 71), 0),
        "group_id": draw_group_id(jax.random.fold_in(seeds[12], 71), 0),
        "slot_of": jax.random.permutation(seeds[5], TILES).astype(jnp.int32),
        "tiles": centred(seeds[6], (TILES, D, D), D ** -0.5, 0.1875, ((0, 8), (1, 4)), jnp.float32),
        "tiles_m": centred(seeds[7], (TILES, D, D), (0.0022 / (TILES * D * D + NVEC * D) ** 0.5), 7.62939453125e-06, ((0, 8), (1, 4)), jnp.float32),
        "tiles_v": jnp.clip(jnp.exp(math.log(4.858807800545151e-12) - 1.3862944 * jax.random.uniform(seeds[8], (TILES, D, D), jnp.float32) ** level_of(seeds[8], (TILES, D, D), ((0, 8), (1, 4)), -0.2, 0.2)), 1.2147019501362877e-12, 4.858807800545151e-12),
        "vectors": draw_vectors(jax.random.fold_in(seeds[12], 71), 0),
        "vec_m": centred(seeds[10], (NVEC, D), (0.0088 / (TILES * D * D + NVEC * D) ** 0.5), 3.0517578125e-05, (), jnp.float32),
        "vec_v": jnp.clip(jnp.exp(jax.random.uniform(seeds[11], (NVEC, D), jnp.float32, math.log(1.9666601680512485e-11), math.log(7.750955433039053e-11))), 1.9666601680512485e-11, 7.750955433039053e-11),
    }


HIGHEST = lax.Precision.HIGHEST
beta_one = 0.9
beta_two = 0.95
clip_norm = 0.02
rate_tiles = 0.01
rate_vectors = 0.1
decay_weight = 1e-05
adam_eps = 1e-08
norm_eps = 1e-05

@jax.custom_vjp
def low(v):
    return lax.optimization_barrier(v.astype(jnp.bfloat16)).astype(jnp.float32)

@jax.custom_vjp
def low_back(v):
    return v

def low_keep(v):
    return (low(v), None)

def low_pass(kept, grad):
    return (grad,)

def back_keep(v):
    return (v, None)

def back_low(kept, grad):
    return (low(grad),)
low.defvjp(low_keep, low_pass)
low_back.defvjp(back_keep, back_low)

def position_table(start, count):
    index = start + jnp.arange(count)
    patch_row = (index // PCOLS).astype(jnp.float32)
    patch_col = (index % PCOLS).astype(jnp.float32)
    quarter = D // 4
    omega = jnp.exp(-math.log(10000.0) * jnp.arange(quarter).astype(jnp.float32) / quarter)
    angle_row = patch_row[:, None] * omega[None, :]
    angle_col = patch_col[:, None] * omega[None, :]
    return jnp.concatenate([jnp.sin(angle_row), jnp.cos(angle_row), jnp.sin(angle_col), jnp.cos(angle_col)], axis=1)

def latitude_table(start, count):
    index = start + jnp.arange(count)
    inner = jnp.arange(PIX) // 2
    lat_rows = 2 * (index // PCOLS)[:, None] + inner[None, :]
    total_rows = 2 * PROWS
    angle = (lat_rows.astype(jnp.float32) + 0.5) * (math.pi / total_rows) - math.pi / 2
    every = (jnp.arange(total_rows).astype(jnp.float32) + 0.5) * (math.pi / total_rows) - math.pi / 2
    weight = jnp.cos(angle) / jnp.mean(jnp.cos(every))
    return jnp.tile(weight, (1, VARS))

def layer_norm(values, gain, shift):
    center = values - lax.optimization_barrier(jnp.mean(values, axis=-1, keepdims=True))
    spread = lax.optimization_barrier(jnp.mean(center * center, axis=-1, keepdims=True))
    return center * lax.rsqrt(spread + norm_eps) * gain + shift

def matmul(inputs, weight):
    return low_back(jnp.dot(low(inputs), low(weight), precision=HIGHEST))

def aggregate(tokens, query_low, weight_key, weight_value, bias_value):
    scale = HD ** (-0.5)

    def block(token_block):
        count = token_block.shape[0]
        keys_var = low(matmul(token_block, weight_key)).reshape(count, VARS, HEADS, HD)
        vals_var = low(matmul(token_block, weight_value) + bias_value).reshape(count, VARS, HEADS, HD)
        score = low_back(jnp.einsum('he,nvhe->nhv', query_low, keys_var, precision=HIGHEST) * scale)
        probs = jax.nn.softmax(score, axis=-1)
        mixed = low_back(jnp.einsum('nhv,nvhe->nhe', low(probs), vals_var, precision=HIGHEST))
        return mixed.reshape(count, D)
    size = min(PATCHES, 256)
    blocks = tokens.reshape(PATCHES // size, size, VARS, D)
    return lax.map(jax.checkpoint(block), blocks).reshape(PATCHES, D)

def attention_rows(query_rows, key_rows, value_rows):
    scale = HD ** (-0.5)

    def block(query_block):
        score = low_back(jnp.einsum('qhe,khe->hqk', query_block, key_rows, precision=HIGHEST) * scale)
        probs = jax.nn.softmax(score, axis=-1)
        return low_back(jnp.einsum('hqk,khe->qhe', low(probs), value_rows, precision=HIGHEST))
    size = min(PATCHES, 512)
    blocks = query_rows.reshape(PATCHES // size, size, HEADS, HD)
    return lax.map(jax.checkpoint(block), blocks).reshape(PATCHES, D)

def sample_loss(tiles_mat, vectors, field, target, mask, lead, sample_weight, count_pixels, latitude):
    folds = FF // D
    offset = VARS * PIX
    embed_weight = vectors[:offset].reshape(VARS, PIX, D)
    embed_bias = vectors[offset:offset + VARS] + vectors[offset + VARS:offset + 2 * VARS]
    head_weight = vectors[offset + 2 * VARS:2 * offset + 2 * VARS]
    extras = vectors[2 * offset + 2 * VARS:]
    tokens = jnp.einsum('pvk,vkd->pvd', field.reshape(PATCHES, VARS, PIX), embed_weight, precision=HIGHEST) + embed_bias[None]
    query_agg = jnp.dot(low(extras[0]), low(tiles_mat[0]), precision=HIGHEST) + extras[3]
    query_low = low(query_agg).reshape(HEADS, HD)
    mixed = aggregate(tokens, query_low, tiles_mat[1], tiles_mat[2], extras[4])
    hidden0 = matmul(mixed, tiles_mat[3]) + extras[5] + position_table(0, PATCHES) + (lead * extras[1] + extras[2])
    normed1 = layer_norm(hidden0, extras[6], extras[7])
    query_rows = low(matmul(normed1, tiles_mat[4]) + extras[8]).reshape(PATCHES, HEADS, HD)
    key_rows = low(matmul(normed1, tiles_mat[5])).reshape(PATCHES, HEADS, HD)
    value_rows = low(matmul(normed1, tiles_mat[6]) + extras[9]).reshape(PATCHES, HEADS, HD)
    attended = attention_rows(query_rows, key_rows, value_rows)
    hidden1 = hidden0 + matmul(attended, tiles_mat[7])
    normed2 = layer_norm(hidden1, extras[10], extras[11])
    weight_one = jnp.transpose(tiles_mat[8:8 + folds], (1, 0, 2)).reshape(D, FF)
    pre_act = matmul(normed2, weight_one) + extras[15:15 + folds].reshape(FF)
    activ = jax.nn.gelu(pre_act, approximate=False)
    weight_two = tiles_mat[8 + folds:].reshape(FF, D)
    hidden2 = hidden1 + matmul(activ, weight_two) + extras[12]
    normed3 = layer_norm(hidden2, extras[13], extras[14])
    predict = matmul(normed3, head_weight.T)
    error = predict - target
    return jnp.sum(sample_weight * mask * latitude * error * error / count_pixels)

def adam_update(weight, grad, first, second, rate):
    first = beta_one * first + (1.0 - beta_one) * grad
    second = beta_two * second + (1.0 - beta_two) * grad * grad
    first_hat = first / (1.0 - beta_one ** STEP)
    second_hat = second / (1.0 - beta_two ** STEP)
    weight = weight - rate * (first_hat / (jnp.sqrt(second_hat) + adam_eps) + decay_weight * weight)
    return (weight, first, second)

def reference(fields, targets, lead_time, pixel_mask, group_id, slot_of, tiles, tiles_m, tiles_v, vectors, vec_m, vec_v):
    tiles_mat = jnp.take(tiles, slot_of, axis=0)
    mask_float = pixel_mask.astype(jnp.float32)
    var_total = lax.optimization_barrier(jnp.sum(mask_float.reshape(SAMPLES, PATCHES, VARS, PIX), axis=(0, 1, 3)))
    count_pixels = VARS * jnp.repeat(var_total, PIX)
    group_hot = (group_id[:, None] == jnp.arange(GROUPS)[None, :]).astype(jnp.float32)
    group_total = lax.optimization_barrier(jnp.sum(group_hot, axis=0))
    sample_weight = SAMPLES / (GROUPS * lax.optimization_barrier(jnp.sum(group_hot * group_total[None, :], axis=1)))
    latitude = latitude_table(0, PATCHES)

    def scan_step(carry, items):
        field, target, mask, lead, weight_s = items

        def loss_of(tiles_arg, vectors_arg):
            return sample_loss(tiles_arg, vectors_arg, field, target, mask, lead, weight_s, count_pixels, latitude)
        value, pull = jax.vjp(loss_of, tiles_mat, vectors)
        grad_tiles, grad_vectors = pull(jnp.ones_like(value))
        return ((carry[0] + value, carry[1] + grad_tiles, carry[2] + grad_vectors), None)
    start = (jnp.zeros((), jnp.float32), jnp.zeros_like(tiles_mat), jnp.zeros_like(vectors))
    (loss, grad_tiles, grad_vectors), _ = lax.scan(scan_step, start, (fields, targets, mask_float, lead_time, sample_weight))
    slot_grads = jnp.take(grad_tiles, jnp.argsort(slot_of), axis=0)
    grad_norm = jnp.sqrt(jnp.sum(slot_grads * slot_grads) + jnp.sum(grad_vectors * grad_vectors))
    clip = jnp.minimum(1.0, clip_norm / (grad_norm + 1e-06))
    tiles_new, tiles_m_new, tiles_v_new = adam_update(tiles, slot_grads * clip, tiles_m, tiles_v, rate_tiles)
    vectors_new, vec_m_new, vec_v_new = adam_update(vectors, grad_vectors * clip, vec_m, vec_v, rate_vectors)
    return (loss, grad_norm, tiles_new, tiles_m_new, tiles_v_new, vectors_new, vec_m_new, vec_v_new)
```

```python
import functools
import math

import jax
import jax.numpy as jnp
from jax import lax
from jax.experimental import pallas as pl
from jax.experimental.pallas import tpu as pltpu
from jax.sharding import PartitionSpec as P

D = 1024
HEADS = 16
HD = 64
FF = 4096
VARS = 48
PIX = 4
TABLE = (PIX + 1) * VARS
norm_eps = 1e-05
f32 = jnp.float32
bf16 = jnp.bfloat16
NT = (((1,), (1,)), ((), ()))
NN = (((1,), (0,)), ((), ()))


def nt(a, b):
    return lax.dot_general(a, b, NT, preferred_element_type=f32)


def nn(a, b):
    return lax.dot_general(a, b, NN, preferred_element_type=f32)


def once(shape):
    zeros = (0,) * len(shape)
    return pl.BlockSpec(shape, lambda *_: zeros, pipeline_mode=pl.Buffered(1))


def cost(flops, moved, exps=0):
    return pl.CostEstimate(flops=flops, bytes_accessed=moved, transcendentals=exps)


def limit(mib):
    return pltpu.CompilerParams(vmem_limit_bytes=mib << 20)


def tile_spec(every, m):
    return pl.BlockSpec(every.shape[:2] + (1,) + every.shape[3:], lambda *_: (0, 0, m, 0, 0), pipeline_mode=pl.Buffered(1))


def tile_of(ref):
    return ref[...].reshape(D, D)


def attend_kernel(qb, q_ref, k_ref, v_ref, o_ref, l_ref):
    rows = q_ref.shape[0]
    lane = lax.broadcasted_iota(jnp.int32, (qb, 128), 1)
    pair = pl.program_id(0)

    @pl.when(pair == 0)
    def _():
        l_ref[...] = jnp.zeros_like(l_ref)

    def step(i, carry):
        at = pl.ds(pl.multiple_of(i * qb, qb), qb)
        q = q_ref[at, :]
        outs = []
        low = l_ref[at, :]
        for h in range(2):
            own = (lane < HD) if h == 0 else (lane >= HD)
            s = nt(jnp.where(own, q, jnp.zeros_like(q)), k_ref[...])
            m = jnp.max(s, axis=1, keepdims=True)
            e = jnp.exp(s - m)
            t = jnp.sum(e, axis=1, keepdims=True)
            outs.append(nn(e.astype(bf16), v_ref[...]) * (1.0 / t))
            low = jnp.where(lane == 2 * pair + h, m + jnp.log(t), low)
        o_ref[at, :] = jnp.where(lane < HD, outs[0], outs[1]).astype(bf16)
        l_ref[at, :] = low
        return carry

    lax.fori_loop(0, rows // qb, step, 0)


def attend(q, k, v, qb=256):
    rows, total = q.shape[0], k.shape[0]
    qb = min(qb, rows)
    pair_q = pl.BlockSpec((rows, 128), lambda p: (0, p))
    pair_k = pl.BlockSpec((total, 128), lambda p: (0, p))
    return pl.pallas_call(
        functools.partial(attend_kernel, qb),
        grid=(HEADS // 2,),
        in_specs=[pair_q, pair_k, pair_k],
        out_specs=[pair_q, pl.BlockSpec((rows, 128), lambda p: (0, 0))],
        out_shape=[jax.ShapeDtypeStruct((rows, D), bf16), jax.ShapeDtypeStruct((rows, 128), f32)],
        compiler_params=limit(48),
        cost_estimate=cost(16 * rows * total * D, 8 * total * D, HEADS * rows * total),
        name="attend",
    )(q, k, v)


def attend_back_kernel(qb, q_ref, k_ref, v_ref, o_ref, g_ref, l_ref, dq_ref, dk_ref, dv_ref, dk_acc, dv_acc):
    rows = q_ref.shape[0]
    lane = lax.broadcasted_iota(jnp.int32, (qb, 128), 1)
    pair = pl.program_id(0)
    dk_acc[...] = jnp.zeros_like(dk_acc)
    dv_acc[...] = jnp.zeros_like(dv_acc)

    def step(i, carry):
        at = pl.ds(pl.multiple_of(i * qb, qb), qb)
        q = q_ref[at, :]
        g = g_ref[at, :]
        qt = q.astype(f32).T.astype(bf16)
        gt = g.astype(f32).T.astype(bf16)
        prod = o_ref[at, :].astype(f32) * g.astype(f32)
        low = l_ref[at, :]
        dqs = []
        for h in range(2):
            own = (lane < HD) if h == 0 else (lane >= HD)
            lse = jnp.sum(jnp.where(lane == 2 * pair + h, low, 0.0), axis=1, keepdims=True)
            delta = jnp.sum(jnp.where(own, prod, 0.0), axis=1, keepdims=True)
            s = nt(jnp.where(own, q, jnp.zeros_like(q)), k_ref[...])
            p = jnp.exp(s - lse)
            dp = nt(jnp.where(own, g, jnp.zeros_like(g)), v_ref[...])
            ds = (p * (dp - delta)).astype(bf16)
            part = pl.ds(h * HD, HD)
            dv_acc[part, :] += nn(gt[h * HD : (h + 1) * HD, :], p.astype(bf16))
            dk_acc[part, :] += nn(qt[h * HD : (h + 1) * HD, :], ds)
            dqs.append(nn(ds, k_ref[...]))
        dq_ref[at, :] = (jnp.where(lane < HD, dqs[0], dqs[1]) * (HD**-0.5)).astype(bf16)
        return carry

    lax.fori_loop(0, rows // qb, step, 0)
    dk_ref[...] = dk_acc[...].T.astype(bf16)
    dv_ref[...] = dv_acc[...].T.astype(bf16)


def attend_back(q, k, v, o, g, l, qb=512):
    rows, total = q.shape[0], k.shape[0]
    qb = min(qb, rows)
    pair_q = pl.BlockSpec((rows, 128), lambda p: (0, p))
    pair_k = pl.BlockSpec((total, 128), lambda p: (0, p))
    return pl.pallas_call(
        functools.partial(attend_back_kernel, qb),
        grid=(HEADS // 2,),
        in_specs=[pair_q, pair_k, pair_k, pair_q, pair_q, pl.BlockSpec((rows, 128), lambda p: (0, 0))],
        out_specs=[pair_q, pair_k, pair_k],
        out_shape=[
            jax.ShapeDtypeStruct((rows, D), bf16),
            jax.ShapeDtypeStruct((total, D), bf16),
            jax.ShapeDtypeStruct((total, D), bf16),
        ],
        scratch_shapes=[pltpu.VMEM((128, total), f32), pltpu.VMEM((128, total), f32)],
        compiler_params=limit(48),
        cost_estimate=cost(40 * rows * total * D, 16 * total * D, HEADS * rows * total),
        name="attend_back",
    )(q, k, v, o, g, l)


def fold_kernel(w0_ref, w1_ref, w2_ref, hi_ref, lo_ref, vec_ref, coef_ref, low_ref, lowt_ref, key_ref, query_ref):
    head = lax.broadcasted_iota(jnp.int32, (128, D), 0)
    column = lax.broadcasted_iota(jnp.int32, (128, D), 1)
    query = (nn(vec_ref[...].astype(bf16), tile_of(w0_ref))[0:1, :] + vec_ref[1:2, :]).astype(bf16)
    query_ref[...] = jnp.broadcast_to(query.astype(f32), query_ref.shape)
    spread = jnp.where(column // HD == head, query.astype(f32), 0.0).astype(bf16)
    key = nt(spread, tile_of(w1_ref)) * (HD**-0.5)
    key_ref[...] = key[:HEADS]
    key_hi = key.astype(bf16)
    key_lo = (key - key_hi.astype(f32)).astype(bf16)
    coef_ref[...] = nt(hi_ref[...], key_hi) + nt(lo_ref[...], key_hi) + nt(hi_ref[...], key_lo)
    value = tile_of(w2_ref)
    val = nn(hi_ref[...], value) + nn(lo_ref[...], value)
    row = lax.broadcasted_iota(jnp.int32, (TABLE, D), 0)
    val = jnp.where(row >= PIX * VARS, val + vec_ref[2:3, :], val)
    low_ref[...] = val.astype(bf16)
    lowt_ref[...] = val.T.astype(bf16)


def fold(every, hi, lo, vecs):
    return pl.pallas_call(
        fold_kernel,
        grid=(1,),
        in_specs=[*(tile_spec(every, m) for m in range(3)), once((TABLE, D)), once((TABLE, D)), once((8, D))],
        out_specs=[once(s) for s in ((TABLE, 128), (TABLE, D), (D, TABLE), (HEADS, D), (8, D))],
        out_shape=[
            jax.ShapeDtypeStruct((TABLE, 128), f32),
            jax.ShapeDtypeStruct((TABLE, D), bf16),
            jax.ShapeDtypeStruct((D, TABLE), bf16),
            jax.ShapeDtypeStruct((HEADS, D), f32),
            jax.ShapeDtypeStruct((8, D), f32),
        ],
        compiler_params=limit(40),
        cost_estimate=cost(6 * TABLE * D * D, 6 * D * D),
        name="fold",
    )(every, every, every, hi, lo, vecs)


def mix_probs(f, coef_ref, h):
    part = lambda k: coef_ref[k * VARS : (k + 1) * VARS, h : h + 1]
    s = part(PIX)
    for k in range(PIX):
        s = s + part(k) * f[k]
    e = jnp.exp(s - jnp.max(s, axis=0, keepdims=True))
    return e * (1.0 / jnp.sum(e, axis=0, keepdims=True))


def mix_kernel(f_ref, coef_ref, tt_ref, o_ref):
    f = [f_ref[0, k].astype(f32) for k in range(PIX)]

    def one(h):
        pa = mix_probs(f, coef_ref, h)
        pf = jnp.concatenate([pa * x for x in f] + [pa], axis=0).astype(bf16)
        return nn(tt_ref[h * HD : (h + 1) * HD, :], pf)

    for p in range(HEADS // 2):
        both = jnp.concatenate([one(2 * p), one(2 * p + 1)], axis=0)
        o_ref[:, p * 128 : (p + 1) * 128] = both.T.astype(bf16)


def mix(fields, coef, tt):
    nb, _, _, count = fields.shape
    return pl.pallas_call(
        mix_kernel,
        grid=(nb,),
        in_specs=[
            pl.BlockSpec((1, PIX, VARS, count), lambda b: (b, 0, 0, 0)),
            once((TABLE, 128)),
            once((D, TABLE)),
        ],
        out_specs=pl.BlockSpec((count, D), lambda b: (b, 0)),
        out_shape=jax.ShapeDtypeStruct((nb * count, D), bf16),
        compiler_params=limit(40),
        cost_estimate=cost(8 * nb * count * TABLE * D, 4 * nb * count * D, nb * count * VARS * HEADS),
        name="mix",
    )(fields, coef, tt)


def mix_back_kernel(side_ref, f_ref, coef_ref, t_ref, g_ref, rest_ref, mine_ref, other_ref, dt_ref, dc_ref):
    @pl.when(pl.program_id(0) == 0)
    def _():
        dc_ref[...] = jnp.zeros_like(dc_ref)
        dt_ref[...] = jnp.zeros_like(dt_ref)

    lane = lax.broadcasted_iota(jnp.int32, (VARS, 128), 1)
    f = [f_ref[0, k].astype(f32) for k in range(PIX)]
    for h in range(HEADS):
        pair = slice(h // 2 * 128, h // 2 * 128 + 128)
        own = (lane[:1] < HD) if h % 2 == 0 else (lane[:1] >= HD)
        pa = mix_probs(f, coef_ref, h)
        pf = jnp.concatenate([pa * x for x in f] + [pa], axis=0).astype(bf16)
        g = jnp.where(own, g_ref[:, pair], jnp.zeros((), bf16))
        dpf = nt(t_ref[:, pair], g)
        dpa = dpf[PIX * VARS :]
        for k in range(PIX):
            dpa = dpa + dpf[k * VARS : (k + 1) * VARS] * f[k]
        ds = pa * (dpa - jnp.sum(pa * dpa, axis=0, keepdims=True))
        for k in range(PIX + 1):
            w = ds * f[k] if k < PIX else ds
            dc_ref[k * VARS : (k + 1) * VARS, :] += jnp.where(lane == h, jnp.sum(w, axis=1, keepdims=True), 0.0)
        dt_ref[:, pair] += nn(pf, g)

    @pl.when(pl.program_id(0) == pl.num_programs(0) - 1)
    def _():
        dct = jnp.concatenate([dc_ref[...].T[:HEADS], jnp.zeros((HEADS, D // 2 - TABLE), f32)], axis=1)
        half = D // 2
        for at, left, right in (
            (0, dt_ref[:, :half], dt_ref[:, half:]),
            (TABLE, dct, jnp.zeros_like(dct)),
            (TABLE + HEADS, rest_ref[:, :half], rest_ref[:, half:]),
        ):
            rows = slice(at, at + left.shape[0])
            first = side_ref[0] == 0
            mine_ref[rows, :] = jnp.where(first, left, right)
            other_ref[rows, :] = jnp.where(first, right, left).astype(bf16)


def mix_back(side, fields, coef, t, g, rest):
    nb, _, _, count = fields.shape
    shape = (TABLE + HEADS + rest.shape[0], D // 2)
    whole = lambda s: pl.BlockSpec(s, lambda b: (0,) * len(s))
    return pl.pallas_call(
        mix_back_kernel,
        grid=(nb,),
        in_specs=[
            pl.BlockSpec(memory_space=pltpu.SMEM),
            pl.BlockSpec((1, PIX, VARS, count), lambda b: (b, 0, 0, 0)),
            once((TABLE, 128)),
            once((TABLE, D)),
            pl.BlockSpec((count, D), lambda b: (b, 0)),
            once(rest.shape),
        ],
        out_specs=[whole(shape), whole(shape)],
        out_shape=[jax.ShapeDtypeStruct(shape, f32), jax.ShapeDtypeStruct(shape, bf16)],
        scratch_shapes=[pltpu.VMEM((TABLE, D), f32), pltpu.VMEM((TABLE, 128), f32)],
        compiler_params=limit(40),
        cost_estimate=cost(16 * nb * count * TABLE * D, 4 * nb * count * D, nb * count * VARS * HEADS),
        name="mix_back",
    )(side, fields, coef, t, g, rest)


def front_kernel(m_ref, w3_ref, w4_ref, w5_ref, w6_ref, row_ref, col_ref, vec_ref, h_ref, a_ref, q_ref, k_ref, v_ref):
    per = row_ref.shape[1]
    h = nn(m_ref[...], tile_of(w3_ref))
    h = h + jnp.concatenate([col_ref[...] + row_ref[0, i : i + 1, :] for i in range(per)], axis=0)
    h_ref[...] = h
    center = h - jnp.mean(h, axis=-1, keepdims=True)
    inverse = lax.rsqrt(jnp.mean(center * center, axis=-1, keepdims=True) + norm_eps)
    a = (center * inverse * vec_ref[0:1, :] + vec_ref[1:2, :]).astype(bf16)
    a_ref[...] = a
    k_ref[...] = nn(a, tile_of(w5_ref)).astype(bf16)
    v_ref[...] = (nn(a, tile_of(w6_ref)) + vec_ref[3:4, :]).astype(bf16)

    @pl.when(pl.program_id(0) == 0)
    def _():
        q_ref[...] = ((nn(a, tile_of(w4_ref)) + vec_ref[2:3, :]) * (HD**-0.5)).astype(bf16)


def front(mixed, every, row, col, vecs, blocks):
    total = mixed.shape[0]
    count = total // blocks
    per = row.shape[0] // blocks
    block = pl.BlockSpec((count, D), lambda b: (b, 0))
    return pl.pallas_call(
        front_kernel,
        grid=(blocks,),
        in_specs=[
            block,
            *(tile_spec(every, m) for m in range(3, 7)),
            pl.BlockSpec((1, per, D), lambda b: (b, 0, 0)),
            once(col.shape),
            once(vecs.shape),
        ],
        out_specs=[block, block, pl.BlockSpec((count, D), lambda b: (0, 0)), block, block],
        out_shape=[
            jax.ShapeDtypeStruct((total, D), f32),
            jax.ShapeDtypeStruct((total, D), bf16),
            jax.ShapeDtypeStruct((count, D), bf16),
            jax.ShapeDtypeStruct((total, D), bf16),
            jax.ShapeDtypeStruct((total, D), bf16),
        ],
        compiler_params=limit(52),
        cost_estimate=cost(6 * total * D * D, 16 * total * D),
        name="front",
    )(mixed, *[every] * 4, row.reshape(blocks, per, D), col, vecs)


def back_kernel(dq_ref, dk_ref, dv_ref, h_ref, dh_ref, w3_ref, w4_ref, w5_ref, w6_ref, vec_ref, g_ref, gm_ref, sum_ref, acc):
    first = pl.program_id(0) == 0
    acc[...] = nt(dk_ref[...], tile_of(w5_ref)) + nt(dv_ref[...], tile_of(w6_ref))

    @pl.when(first)
    def _():
        sum_ref[...] = jnp.zeros_like(sum_ref)
        acc[...] += nt(dq_ref[...], tile_of(w4_ref))
        sum_ref[4:5, :] = jnp.sum(dq_ref[...].astype(f32), axis=0, keepdims=True)

    h = h_ref[...]
    center = h - jnp.mean(h, axis=-1, keepdims=True)
    inverse = lax.rsqrt(jnp.mean(center * center, axis=-1, keepdims=True) + norm_eps)
    normed = center * inverse
    grad = acc[...]
    sum_ref[1:2, :] += jnp.sum(grad * normed, axis=0, keepdims=True)
    sum_ref[2:3, :] += jnp.sum(grad, axis=0, keepdims=True)
    sum_ref[3:4, :] += jnp.sum(dv_ref[...].astype(f32), axis=0, keepdims=True)
    scaled = grad * vec_ref[0:1, :]
    out = inverse * (
        scaled
        - jnp.mean(scaled, axis=-1, keepdims=True)
        - normed * jnp.mean(scaled * normed, axis=-1, keepdims=True)
    )
    acc[...] = out

    @pl.when(first)
    def _():
        acc[...] += dh_ref[...]

    out = acc[...]
    sum_ref[0:1, :] += jnp.sum(out, axis=0, keepdims=True)
    low = out.astype(bf16)
    g_ref[...] = low
    gm_ref[...] = nt(low, tile_of(w3_ref)).astype(bf16)


def back(dq, dk, dv, h, dh, every, vecs, blocks):
    total = dk.shape[0]
    count = total // blocks
    block = pl.BlockSpec((count, D), lambda b: (b, 0))
    return pl.pallas_call(
        back_kernel,
        grid=(blocks,),
        in_specs=[
            once((count, D)),
            block,
            block,
            block,
            once((count, D)),
            *(tile_spec(every, m) for m in range(3, 7)),
            once(vecs.shape),
        ],
        out_specs=[block, block, pl.BlockSpec((8, D), lambda b: (0, 0))],
        out_shape=[
            jax.ShapeDtypeStruct((total, D), bf16),
            jax.ShapeDtypeStruct((total, D), bf16),
            jax.ShapeDtypeStruct((8, D), f32),
        ],
        scratch_shapes=[pltpu.VMEM((count, D), f32)],
        compiler_params=limit(52),
        cost_estimate=cost(7 * total * D * D, 16 * total * D),
        name="back",
    )(dq, dk, dv, h, dh, *[every] * 4, vecs)


def choose_kernel(first, slot_ref, p_ref, wait_ref, out_ref):
    for m in range(out_ref.shape[0]):
        out_ref[m] = p_ref[slot_ref[first + m]]


def choose(slot_of, pieces, first, count, wait):
    shape = (count,) + pieces.shape[1:]
    whole = lambda s: pl.BlockSpec(s, lambda i, at: (0, 0, 0))
    return pl.pallas_call(
        functools.partial(choose_kernel, first),
        grid_spec=pltpu.PrefetchScalarGridSpec(
            num_scalar_prefetch=1,
            grid=(1,),
            in_specs=[whole(pieces.shape), pl.BlockSpec(memory_space=pl.ANY)],
            out_specs=whole(shape),
        ),
        out_shape=jax.ShapeDtypeStruct(shape, pieces.dtype),
        compiler_params=limit(32),
        cost_estimate=cost(0, 4 * pieces.size),
        name="choose",
    )(slot_of, pieces, wait)


def finish_kernel(plan, slot_ref, *refs):
    ins, out, square = refs[:-2], refs[-2], refs[-1]
    half = out.shape[2]
    for m in range(3):
        out[slot_ref[m]] = jnp.zeros_like(out[0])
    total = jnp.zeros(out.shape[1:], f32)
    ins = list(ins)
    for per, tiles in plan:
        job, ins = ins[:per], ins[per:]
        for m, index, col in tiles:
            parts = [r[index, :, col * half : (col + 1) * half].astype(f32) for r in job]
            value = sum(parts[1:], parts[0])
            out[slot_ref[m]] = value.astype(out.dtype)
            total = total + value * value
    square[...] = jnp.sum(total.reshape(total.shape[0] // 8, 8, half), axis=0)


def finish(slot_of, plan, jobs):
    arrays = [a for job in jobs for a in job]
    plan = tuple((len(job), tiles) for job, tiles in zip(jobs, plan))
    rows, half = arrays[0].shape[1], D // 2
    whole = lambda s: pl.BlockSpec(s, lambda i, at: (0,) * len(s))
    n = slot_of.shape[0]
    return pl.pallas_call(
        functools.partial(finish_kernel, plan),
        grid_spec=pltpu.PrefetchScalarGridSpec(
            num_scalar_prefetch=1,
            grid=(1,),
            in_specs=[whole(a.shape) for a in arrays],
            out_specs=[whole((n, rows, half)), whole((8, half))],
        ),
        out_shape=[jax.ShapeDtypeStruct((n, rows, half), bf16), jax.ShapeDtypeStruct((8, half), f32)],
        compiler_params=limit(48),
        cost_estimate=cost(0, 3 * 4 * n * rows * half),
        name="finish",
    )(slot_of, *arrays)


beta_one = 0.9
beta_two = 0.95
rate_tiles = 0.01
rate_vectors = 0.1
decay_weight = 1e-05
adam_eps = 1e-08
STEP = 10
clip_norm = 0.02


def adam_update(weight, grad, first, second, rate):
    first = beta_one * first + (1.0 - beta_one) * grad
    second = beta_two * second + (1.0 - beta_two) * grad * grad
    first_hat = first / (1.0 - beta_one**STEP)
    second_hat = second / (1.0 - beta_two**STEP)
    weight = weight - rate * (first_hat / (jnp.sqrt(second_hat) + adam_eps) + decay_weight * weight)
    return (weight, first, second)


def tail_kernel(square_ref, w0_ref, w1_ref, w2_ref, hi_ref, lo_ref, gram_ref, key_ref, query_ref, vec_ref, late_ref,
                p_ref, m_ref, v_ref, clip_ref, gkey_ref, agg_ref, p_new, m_new, v_new, ge, extra):
    head = lax.broadcasted_iota(jnp.int32, (HEADS, D), 0)
    column = lax.broadcasted_iota(jnp.int32, (HEADS, D), 1)

    def parts(a):
        high = a.astype(bf16)
        return high, (a - high.astype(f32)).astype(bf16)

    def tn(a, b):
        return lax.dot_general(a, b, (((0,), (0,)), ((), ())), preferred_element_type=f32)

    offset = PIX * VARS
    fold_ref, head_ref = late_ref.at[0:TABLE, :], late_ref.at[TABLE + 40 : TABLE + 40 + offset, :]
    coef_hi, coef_lo = parts(late_ref[TABLE : TABLE + HEADS, 0:256][:, :TABLE])
    grad_key = (nn(coef_hi, hi_ref[...]) + nn(coef_hi, lo_ref[...]) + nn(coef_lo, hi_ref[...])) * (HD**-0.5)
    gkey_ref[...] = grad_key
    key_hi, key_lo = parts(grad_key)
    by_head = nn(key_hi, tile_of(w1_ref)) + nn(key_lo, tile_of(w1_ref))
    agg = jnp.sum(jnp.where(column // HD == head, by_head, 0.0), axis=0, keepdims=True)
    agg_ref[...] = jnp.broadcast_to(agg, agg_ref.shape)
    agg_hi, agg_lo = parts(jnp.broadcast_to(agg, (8, D)))
    by_query = (nt(agg_hi, tile_of(w0_ref)) + nt(agg_lo, tile_of(w0_ref)))[0:1]
    fold_hi, fold_lo = parts(fold_ref[...])
    fold_key_hi, fold_key_lo = parts(key_ref[...])
    ge[...] = (
        nt(fold_hi, tile_of(w2_ref)) + nt(fold_lo, tile_of(w2_ref))
        + tn(coef_hi, fold_key_hi) + tn(coef_hi, fold_key_lo) + tn(coef_lo, fold_key_hi)
    )
    rest = late_ref[TABLE + HEADS : TABLE + HEADS + 24, :]
    order = [
        by_query, rest[5:6], rest[0:1], agg, jnp.sum(fold_ref[offset:, :], axis=0, keepdims=True), rest[0:1],
        rest[1:2], rest[2:3], rest[4:5], rest[3:4], rest[11:12], rest[12:13], rest[8:9], rest[9:10], rest[10:11],
    ]
    for i, r in enumerate(order):
        extra[i : i + 1, :] = r
    extra[15:19, :] = rest[14:18]
    gram_hi, gram_lo = parts(gram_ref[...])
    through = nn(gram_hi, fold_hi) + nn(gram_hi, fold_lo) + nn(gram_lo, fold_hi)
    total = jnp.sum(through * fold_ref[...], axis=0, keepdims=True)
    total += jnp.sum(ge[...] * ge[...], axis=0, keepdims=True)
    bias = ge[offset:, :]
    total += jnp.sum(bias * bias, axis=0, keepdims=True)
    total += jnp.sum(head_ref[...] * head_ref[...], axis=0, keepdims=True)
    total += jnp.sum(extra[0:19, :] * extra[0:19, :], axis=0, keepdims=True)
    vq = vec_ref[0:1, :].astype(bf16).astype(f32)
    total = jnp.sum(total, axis=1, keepdims=True)
    total += jnp.sum(vq * vq, axis=1, keepdims=True) * jnp.sum(agg * agg, axis=1, keepdims=True)
    query = query_ref[0:1, :]
    per_head = jnp.sum(jnp.where(column // HD == head, query * query, 0.0), axis=1, keepdims=True)
    total += jnp.sum(jnp.sum(grad_key * grad_key, axis=1, keepdims=True) * per_head, axis=0, keepdims=True)
    norm = jnp.sqrt(total + square_ref[0])
    clip = jnp.minimum(1.0, clip_norm / (norm + 1e-06))
    lane = lax.broadcasted_iota(jnp.int32, (8, 128), 1)
    clip_ref[...] = jnp.where(lane == 0, clip, norm)

    def update(rows, grad):
        p_new[rows, :], m_new[rows, :], v_new[rows, :] = adam_update(
            p_ref[rows, :], grad * clip, m_ref[rows, :], v_ref[rows, :], rate_vectors
        )

    for k in range(PIX):
        for v in range(VARS):
            extra_row = 32 + v * PIX + k
            extra[extra_row : extra_row + 1, :] = ge[k * VARS + v : k * VARS + v + 1, :]
    update(pl.ds(0, offset), extra[32 : 32 + offset, :])
    update(pl.ds(offset, VARS), bias)
    update(pl.ds(offset + VARS, VARS), bias)
    update(pl.ds(offset + 2 * VARS, offset), head_ref[...])
    update(pl.ds(2 * offset + 2 * VARS, 19), extra[0:19, :])


def tail(square, every, hi, lo, gram, key, query, vecs, late, w, m, v):
    vmem = pl.BlockSpec(memory_space=pltpu.VMEM)
    arrays = (hi, lo, gram, key, query, vecs, late, w, m, v)
    return pl.pallas_call(
        tail_kernel,
        grid=(1,),
        in_specs=[pl.BlockSpec(memory_space=pltpu.SMEM), *(tile_spec(every, m) for m in range(3))]
        + [once(a.shape) for a in arrays],
        out_specs=[once(s) for s in ((8, 128), (HEADS, D), (8, D), w.shape, w.shape, w.shape)],
        out_shape=[
            jax.ShapeDtypeStruct(s, f32) for s in ((8, 128), (HEADS, D), (8, D), w.shape, w.shape, w.shape)
        ],
        scratch_shapes=[pltpu.VMEM((TABLE, D), f32), pltpu.VMEM((32 + PIX * VARS, D), f32)],
        compiler_params=limit(52),
        cost_estimate=cost(8 * TABLE * D * D, 28 * w.size),
        name="tail",
    )(square, every, every, every, *arrays)


PROWS = 32
PCOLS = 64
GROUPS = 5
HIGHEST = lax.Precision.HIGHEST
clip_norm = 0.02
SCALE = HD**-0.5


def position_parts():
    quarter = D // 4
    omega = jnp.exp(-math.log(10000.0) * jnp.arange(quarter).astype(f32) / quarter)
    row = jnp.arange(PROWS).astype(f32)[:, None] * omega[None, :]
    col = jnp.arange(PCOLS).astype(f32)[:, None] * omega[None, :]
    zero_row = jnp.zeros((PROWS, D // 2), f32)
    zero_col = jnp.zeros((PCOLS, D // 2), f32)
    row_part = jnp.concatenate([jnp.sin(row), jnp.cos(row), zero_row], axis=1)
    col_part = jnp.concatenate([zero_col, jnp.sin(col), jnp.cos(col)], axis=1)
    return row_part, col_part


def latitude_table(start, count):
    index = start + jnp.arange(count)
    inner = jnp.arange(PIX) // 2
    lat_rows = 2 * (index // PCOLS)[:, None] + inner[None, :]
    total_rows = 2 * PROWS
    angle = (lat_rows.astype(f32) + 0.5) * (math.pi / total_rows) - math.pi / 2
    every = (jnp.arange(total_rows).astype(f32) + 0.5) * (math.pi / total_rows) - math.pi / 2
    weight = jnp.cos(angle) / jnp.mean(jnp.cos(every))
    return jnp.tile(weight, (1, VARS))


def tn(left, right):
    return lax.dot_general(left, right, (((0,), (0,)), ((), ())), preferred_element_type=f32)


def layer_norm(values, gain, shift):
    center = values - jnp.mean(values, axis=-1, keepdims=True)
    inverse = lax.rsqrt(jnp.mean(center * center, axis=-1, keepdims=True) + norm_eps)
    normed = center * inverse
    return (normed * gain + shift, normed, inverse)


def norm_back(grad_out, normed, inverse, gain):
    scaled = grad_out * gain
    grad_in = inverse * (
        scaled
        - jnp.mean(scaled, axis=-1, keepdims=True)
        - normed * jnp.mean(scaled * normed, axis=-1, keepdims=True)
    )
    return (grad_in, jnp.sum(grad_out * normed, axis=0), jnp.sum(grad_out, axis=0))


def gelu_parts(pre_act):
    phi = 0.5 * (1.0 + lax.erf(pre_act * 0.7071067811865476))
    slope = phi + pre_act * jnp.exp(-0.5 * pre_act * pre_act) * 0.3989422804014327
    return pre_act * phi, slope


def split_low(values):
    high = lax.reduce_precision(values, 8, 7)
    return high.astype(bf16), (values - high).astype(bf16)


def swap(array, bit):
    n = lax.axis_size("dp")
    return lax.ppermute(array, "dp", [(i, i ^ bit) for i in range(n)])


def shift(array, step):
    n = lax.axis_size("blk")
    return lax.ppermute(array, "blk", [(i, (i + step) % n) for i in range(n)])


def dp_bits():
    return [1 << i for i in range(lax.axis_size("dp").bit_length() - 1)]


def after(array, *others):
    return lax.optimization_barrier((array, *others))[0]


def pick(array, axis, index):
    return lax.dynamic_index_in_dim(array, index, axis, False)


def halves(array, side):
    half = array.shape[-1] // 2
    left, right = array[..., :half], array[..., half:]
    return jnp.where(side == 0, left, right), jnp.where(side == 0, right, left)


def sum_small(values):
    n_dp, blocks = lax.axis_size("dp"), lax.axis_size("blk")
    me = lax.axis_index("blk") * n_dp + lax.axis_index("dp")
    width = -(-n_dp * blocks // 128) * 128
    array = jnp.where(jnp.arange(width)[None, :] == me, values[:, None], 0.0)
    array = sum([shift(array, k) for k in range(1, blocks)], array)
    array = sum([swap(array, 2 * mask) for mask in range(1, n_dp // 2)], array)
    return jnp.sum(array + swap(array, 1), axis=1)


def gather_blocks(array):
    n = lax.axis_size("blk")
    return jnp.stack([array] + [shift(array, k) for k in range(1, n)])


def place_kernel(ref, out):
    rows = ref.shape[3]
    for d in range(ref.shape[1]):
        for m in range(ref.shape[2]):
            if len(out.shape) == 2:
                out[d * rows : (d + 1) * rows, m * D : (m + 1) * D] = ref[0, d, m]
            else:
                out[m, d * rows : (d + 1) * rows, :] = ref[0, d, m]


def gather(pieces):
    blocks, n_dp = lax.axis_size("blk"), lax.axis_size("dp")
    return lax.all_gather(pieces, ("blk", "dp"), axis=0).reshape((blocks, n_dp) + pieces.shape)


def place(every, first, size, wide=False):
    blocks, n_dp, _, rows, _ = every.shape
    tall = D // blocks
    at = first // size
    if wide:
        spec, shape = pl.BlockSpec((tall, size * D), lambda z: (z, 0)), (D, size * D)
    else:
        spec, shape = pl.BlockSpec((size, tall, D), lambda z: (0, z, 0)), (size, D, D)
    return pl.pallas_call(
        place_kernel,
        grid=(blocks,),
        in_specs=[pl.BlockSpec((1, n_dp, size, rows, D), lambda z: (z, 0, at, 0, 0))],
        out_specs=spec,
        out_shape=jax.ShapeDtypeStruct(shape, bf16),
        compiler_params=limit(32),
        cost_estimate=cost(0, 4 * size * D * D),
        name="place",
    )(every)


class SplitSum:
    def __init__(self, cur, order, low=True):
        self.blocks = lax.axis_size("blk")
        self.left = list(reversed(dp_bits()[1:]))
        rows = cur.shape[1] // (self.blocks << len(self.left))
        self.cur = cur.reshape((cur.shape[0], self.blocks) + (2,) * len(self.left) + (rows,) + cur.shape[2:])
        self.order = list(order)
        self.type = bf16 if low else f32
        self.got = []

    @classmethod
    def joined(cls, jobs):
        job = cls.__new__(cls)
        for other in jobs:
            other.take()
        job.blocks, job.type, job.got = jobs[0].blocks, jobs[0].type, []
        job.cur = jnp.concatenate([other.cur for other in jobs], axis=0)
        return job

    def take(self):
        for got in self.got:
            self.cur = self.cur + got.astype(f32)
        self.got = []

    def send(self):
        self.take()
        bit = self.order.pop(0)
        axis = 2 + self.left.index(bit)
        mine = (lax.axis_index("dp") // bit) % 2
        sent = pick(self.cur, axis, 1 - mine).astype(self.type)
        self.cur = pick(self.cur, axis, mine)
        self.left.remove(bit)
        self.got = [swap(sent, bit)]
        return sent

    def send_all(self):
        self.take()
        order, n, at = self.order, 1 << len(self.left), 2
        own = lax.axis_index("dp") // 2
        cur = self.cur.reshape(self.cur.shape[:2] + (n,) + self.cur.shape[2 + len(self.left) :])
        sent = [pick(cur, at, own ^ mask).astype(self.type) for mask in range(1, n)]
        self.cur, self.order, self.left = pick(cur, at, own), [], []
        self.got = [swap(a, 2 * (i + 1)) for i, a in enumerate(sent)]
        return sent

    def send_blocks(self):
        self.take()
        blk = lax.axis_index("blk")
        sent = [pick(self.cur, 1, (blk + k) % self.blocks).astype(self.type) for k in range(1, self.blocks)]
        self.cur = pick(self.cur, 1, blk)
        self.got = [shift(a, k + 1) for k, a in enumerate(sent)]
        return sent

    def parts(self):
        return [self.cur, *self.got]

    def end(self):
        for got in self.got:
            self.cur = self.cur + got.astype(f32)
        self.got = []
        return self.cur


class SumRows:
    def __init__(self, mine, other):
        self.rows = mine.shape[0]
        self.side = lax.axis_index("dp") % 2
        self.job = SplitSum((mine + swap(other, 1).astype(f32))[None], dp_bits()[1:])
        self.steps = [self.job.send_all, self.job.send_blocks, self.widen_blocks, self.widen, self.close]

    def step(self):
        return self.steps.pop(0)()

    def widen_blocks(self):
        part = self.job.end()[0].astype(bf16)
        n, blk = lax.axis_size("blk"), lax.axis_index("blk")
        cur = gather_blocks(part)
        self.cur = jnp.stack([pick(cur, 0, (blk - z + n) % n) for z in range(n)])

    def widen(self):
        n, own = lax.axis_size("dp") // 2, lax.axis_index("dp") // 2
        every = jnp.stack([self.cur] + [swap(self.cur, 2 * mask) for mask in range(1, n)])
        self.cur = jnp.stack([pick(every, 0, own ^ i) for i in range(n)], axis=1).reshape(self.rows, -1)

    def close(self):
        cur, got = self.cur, swap(self.cur, 1)
        whole = jnp.where(self.side == 0, jnp.concatenate([cur, got], 1), jnp.concatenate([got, cur], 1))
        return whole.astype(f32)

    def end(self):
        while len(self.steps) > 1:
            self.step()
        return self.step()


def shards(fields, targets, lead_time, pixel_mask, group_id, slot_of, tiles, tiles_m, tiles_v, vectors, vec_m, vec_v):
    _, count, _ = fields.shape
    blocks, n_dp = lax.axis_size("blk"), lax.axis_size("dp")
    total = count * blocks
    folds = FF // D
    dp, blk = lax.axis_index("dp"), lax.axis_index("blk")
    side = dp % 2
    start = blk * count
    others = dp_bits()[1:]
    first_order, second_order = tuple(others), tuple(reversed(others))
    slots, tall, _ = tiles.shape
    n_tiles = slots * n_dp
    rows = 2 * tall // n_dp
    half = D // 2
    fine = tall // n_dp % 16 == 0

    mask_float = pixel_mask[0].astype(f32)
    var_local = jnp.sum(jnp.sum(mask_float, axis=0).reshape(VARS, PIX), axis=1)
    group_hot = (group_id[0] == jnp.arange(GROUPS)).astype(f32)
    counted = sum_small(jnp.pad(jnp.concatenate([var_local, group_hot]), (0, 64 - VARS - GROUPS)))
    field_t = fields[0].astype(bf16).reshape(count, VARS, PIX).transpose(2, 1, 0)
    field_all = gather_blocks(field_t)

    if fine:
        low_rows = tall // n_dp
        pieces = tiles.astype(bf16).reshape(slots, n_dp, low_rows, D)
        pieces = lax.all_to_all(pieces, "dp", 1, 0, tiled=True).reshape(n_tiles, low_rows, D)
        first = gather(choose(slot_of, pieces, 0, 8, slot_of))
        weight_out = place(first, 7, 1)[0]
    else:
        slots_low = lax.all_gather(tiles.astype(bf16), "blk", axis=1, tiled=True)
        slots_low = lax.all_gather(slots_low, "dp", axis=0, tiled=True)
        weights = [pick(slots_low, 0, slot_of[m]) for m in range(n_tiles)]
        first = jnp.stack(weights[:8])[None, None]
        weight_out = weights[7]
        weight_one = jnp.concatenate(weights[8:12], axis=1)
        weight_two = jnp.concatenate(weights[12:], axis=0)

    var_total, group_total = counted[:VARS], counted[VARS : VARS + GROUPS] / blocks
    sample_weight = jnp.sum(group_total) / (GROUPS * jnp.sum(group_hot * group_total))
    count_pixels = VARS * jnp.repeat(var_total, PIX)
    factor = sample_weight * mask_float * latitude_table(start, count) / count_pixels

    offset = VARS * PIX
    embed_weight = vectors[:offset].reshape(VARS, PIX, D).transpose(1, 0, 2).reshape(offset, D)
    embed_bias = vectors[offset : offset + VARS] + vectors[offset + VARS : offset + 2 * VARS]
    embed = jnp.concatenate([embed_weight, embed_bias], axis=0)
    head_low = vectors[offset + 2 * VARS : 2 * offset + 2 * VARS].astype(bf16)
    extras = vectors[2 * offset + 2 * VARS :]
    gram = lax.dot_general(embed, embed, NT, precision=HIGHEST, preferred_element_type=f32)
    embed_hi, embed_lo = split_low(embed)

    fold_vecs = jnp.concatenate([extras[0:1], extras[3:5], jnp.zeros((5, D), f32)], axis=0)
    fold_vecs = after(fold_vecs, counted, field_all[:, 0, :8, :128])
    coef, fold_low, fold_low_t, fold_key, query_f = fold(first, embed_hi, embed_lo, fold_vecs)
    if fine:
        second = gather(choose(slot_of, pieces, 8, 8, first))
        weight_one, weight_two = place(second, 0, 4, True), place(second, 4, 4).reshape(FF, D)
    mixed = mix(field_all, coef, fold_low_t)

    row_part, col_part = position_parts()
    row_part = row_part.reshape(blocks, PROWS // blocks, D)
    row_here = jnp.concatenate([pick(row_part, 0, (blk - k + blocks) % blocks) for k in range(blocks)], axis=0)
    lead_row = extras[5] + lead_time[0] * extras[1] + extras[2]
    vecs = jnp.concatenate([extras[6:10], jnp.zeros((4, D), f32)], axis=0)
    hidden0, normed1_low, query_blk, key_all, value_all = front(
        mixed, first, row_here + lead_row, col_part, vecs, blocks
    )
    own1_low = normed1_low[:count]
    attended_low, log_total = attend(query_blk, key_all, value_all)

    hidden1 = hidden0[:count] + nn(attended_low, weight_out)
    normed2_out, normed2, inverse2 = layer_norm(hidden1, extras[10], extras[11])
    normed2_low = normed2_out.astype(bf16)
    pre_act = nn(normed2_low, weight_one) + extras[15 : 15 + folds].reshape(FF)
    activ, slope = gelu_parts(pre_act)
    activ_low = activ.astype(bf16)
    hidden2 = hidden1 + nn(activ_low, weight_two) + extras[12]
    normed3_out, normed3, inverse3 = layer_norm(hidden2, extras[13], extras[14])
    normed3_low = normed3_out.astype(bf16)
    error = nt(normed3_low, head_low) - targets[0]
    loss_local = jnp.sum(factor * error * error)
    grad_pred_low = (2.0 * factor * error).astype(bf16)
    grad_head = tn(grad_pred_low, normed3_low)
    grad_h2, gain3, shift3 = norm_back(nn(grad_pred_low, head_low), normed3, inverse3, extras[13])
    grad_h2_low = grad_h2.astype(bf16)
    bias2 = jnp.sum(grad_h2, axis=0)
    grad_pre = nt(grad_h2_low, weight_two) * slope
    bias1 = jnp.sum(grad_pre, axis=0).reshape(folds, D)
    grad_pre_low = grad_pre.astype(bf16)

    def weight_grads(left, mine, other):
        sent = tn(left, other).astype(bf16)
        return tn(left, mine), swap(sent, 1), sent

    both = lambda parts: parts[0] + parts[1].astype(f32)
    if fine:
        two_parts = weight_grads(activ_low, *halves(grad_h2_low, side))
        left, right = [
            jnp.concatenate([grad_pre_low[:, f * D + s * half : f * D + (s + 1) * half] for f in range(folds)], axis=1)
            for s in range(2)
        ]
        one_parts = weight_grads(normed2_low, jnp.where(side == 0, left, right), jnp.where(side == 0, right, left))
        two_job = SplitSum(both(two_parts).reshape(folds, D, half), first_order)
        one_job = SplitSum(both(one_parts)[None], second_order)
    grad_n2 = nt(grad_pre_low, weight_one)
    grad_h1_norm, gain2, shift2 = norm_back(grad_n2, normed2, inverse2, extras[10])
    grad_h1 = grad_h2 + grad_h1_norm
    grad_h1_low = grad_h1.astype(bf16)
    early = jnp.concatenate(
        [jnp.stack([bias2, gain3, shift3, gain2, shift2, jnp.zeros_like(bias2)]), bias1, jnp.zeros((6, D), f32), grad_head],
        axis=0,
    )
    grad_attended = nt(grad_h1_low, weight_out).astype(bf16)
    if fine:
        grad_attended = after(grad_attended, two_job.send(), one_job.send(), early)
    grad_query, grad_keys, grad_values = attend_back(query_blk, key_all, value_all, attended_low, grad_attended, log_total)
    if fine:
        sent = [two_job.send(), one_job.send()]
        grad_query, grad_keys, grad_values, *_ = lax.optimization_barrier((grad_query, grad_keys, grad_values, *sent))
        query_parts = weight_grads(own1_low, *halves(grad_query, side))
        out_parts = weight_grads(attended_low, *halves(grad_h1_low, side))
        key_parts = weight_grads(normed1_low, *halves(grad_keys, side))
        value_parts = weight_grads(normed1_low, *halves(grad_values, side))
        pair_job = SplitSum(jnp.stack([both(key_parts), both(value_parts)]), second_order)
        end_job = SplitSum(jnp.stack([both(query_parts), both(out_parts)]), first_order)
        grad_query = after(grad_query, pair_job.send(), end_job.send())
    grad_h0_low, grad_mixed, sums = back(grad_query, grad_keys, grad_values, hidden0, grad_h1, first, vecs, blocks)
    sums = jnp.where(jnp.arange(8)[:, None] == 5, sums[0] * lead_time[0], sums)
    step = 16 * (n_dp // 2) * blocks
    below = sums.shape[0] + early.shape[0]
    rest = jnp.concatenate([sums, early, jnp.zeros((-(TABLE + HEADS + below) % step, D), f32)], axis=0)
    if fine:
        sent = [pair_job.send(), end_job.send(), *two_job.send_blocks(), *one_job.send_blocks(), rest]
        grad_h0_low, grad_mixed, *_, rest = lax.optimization_barrier((grad_h0_low, grad_mixed, *sent))
        agg_parts = weight_grads(mixed, *halves(grad_h0_low, side))
        agg_job = SplitSum(both(agg_parts)[None], first_order)
        grad_mixed = after(grad_mixed, agg_parts[2])
    late_mine, late_other = mix_back(side.reshape(1), field_all, coef, fold_low, grad_mixed, rest)
    if fine:
        late_mine, late_other, *_ = lax.optimization_barrier((late_mine, late_other, *agg_job.send_all()))
    late_job = SumRows(late_mine, late_other)
    if fine:
        edge_job = SplitSum.joined([end_job, pair_job])
        sent = [*edge_job.send_blocks(), two_job.end(), one_job.end()]
        late_job.job.cur = after(late_job.job.cur, *sent)
        late_job.step()
        agg_job.send_blocks()
        plan = (
            [(12 + f, f, 0) for f in range(folds)],
            [(8 + f, 0, f) for f in range(folds)],
            [(m, i, 0) for i, m in enumerate((4, 7, 5, 6))],
            [(3, 0, 0)],
        )
        by_slot, square = finish(slot_of, plan, [j.parts() for j in (two_job, one_job, edge_job, agg_job)])
        part_square = jnp.sum(square)
        while len(late_job.steps) > 1:
            late_job.step()
        by_slot, late_job.cur = lax.optimization_barrier((by_slot, late_job.cur))
        by_slot = lax.all_to_all(by_slot, "dp", 0, 0, tiled=True).astype(f32)
        slot_grads = by_slot.reshape(n_dp // 2, 2, slots, rows, half).transpose(2, 0, 3, 1, 4).reshape(slots, tall, D)
    else:
        rest = [tn(mixed, grad_h0_low), tn(own1_low, grad_query), tn(normed1_low, grad_keys),
                tn(normed1_low, grad_values), tn(attended_low, grad_h1_low)]
        rest += [tn(normed2_low, grad_pre_low[:, f * D : (f + 1) * D]) for f in range(folds)]
        rest += [tn(activ_low[:, f * D : (f + 1) * D], grad_h2_low) for f in range(folds)]
        by_slot = jnp.zeros((n_tiles, D, D), f32)
        for m, grad in enumerate(rest):
            by_slot = lax.dynamic_update_index_in_dim(by_slot, grad, slot_of[m + 3], 0)
        slot_grads = lax.psum_scatter(by_slot, "dp", scatter_dimension=0, tiled=True)
        slot_grads = lax.psum_scatter(slot_grads, "blk", scatter_dimension=1, tiled=True)
        part_square = jnp.sum(slot_grads * slot_grads)
    late = late_job.end()
    numbers = sum_small(jnp.pad(jnp.stack([part_square, loss_local]), (0, 6)))
    loss = numbers[1]
    clips, grad_key, grad_agg, vectors_new, vec_m_new, vec_v_new = tail(
        numbers[:1], first, embed_hi, embed_lo, gram, fold_key, query_f, fold_vecs, late, vectors, vec_m, vec_v
    )
    clip, grad_norm = clips[0, 0], clips[0, 1]

    at_rows = blk * tall
    var_query_f = extras[0].astype(bf16).astype(f32)
    own_first = lax.dynamic_slice_in_dim(var_query_f, at_rows, tall, 0)[:, None] * grad_agg[0][None, :]
    own_key = lax.dynamic_slice_in_dim(grad_key, at_rows, tall, 1)
    own_second = jnp.repeat(own_key.T, HD, axis=1) * query_f[0][None, :]
    own_third = lax.dot_general(
        lax.dynamic_slice_in_dim(embed, at_rows, tall, 1), late[:TABLE], (((0,), (0,)), ((), ())),
        precision=HIGHEST, preferred_element_type=f32,
    )
    my_tiles = [jnp.sum(jnp.where(slot_of == dp * slots + t, jnp.arange(n_tiles), 0)) for t in range(slots)]
    shard_grads = jnp.stack(
        [
            jnp.where(m == 0, own_first, jnp.where(m == 1, own_second, jnp.where(m == 2, own_third, slot_grads[t])))
            for t, m in enumerate(my_tiles)
        ]
    )
    tiles_new, tiles_m_new, tiles_v_new = adam_update(tiles, shard_grads * clip, tiles_m, tiles_v, rate_tiles)
    return (loss, grad_norm, tiles_new, tiles_m_new, tiles_v_new, vectors_new, vec_m_new, vec_v_new)


def solution(mesh):
    tile = P("dp", "blk", None)
    placed = (tile, tile, P("dp"), tile, P("dp"), P(), tile, tile, tile, P(), P(), P())
    return jax.shard_map(
        shards,
        mesh=mesh,
        in_specs=placed,
        out_specs=(P(), P(), tile, tile, tile, P(), P(), P()),
        check_vma=False,
    )
```

```python
import functools
import math

import jax
import jax.numpy as jnp
from jax import lax
from jax.experimental import pallas as pl
from jax.experimental.pallas import tpu as pltpu
from jax.sharding import PartitionSpec as P

D = 1024
HEADS = 16
HD = 64
FF = 4096
VARS = 48
PIX = 4
TABLE = (PIX + 1) * VARS
norm_eps = 1e-05
f32 = jnp.float32
bf16 = jnp.bfloat16
NT = (((1,), (1,)), ((), ()))
NN = (((1,), (0,)), ((), ()))


def nt(a, b):
    return lax.dot_general(a, b, NT, preferred_element_type=f32)


def nn(a, b):
    return lax.dot_general(a, b, NN, preferred_element_type=f32)


def once(shape):
    zeros = (0,) * len(shape)
    return pl.BlockSpec(shape, lambda *_: zeros, pipeline_mode=pl.Buffered(1))


def cost(flops, moved, exps=0):
    return pl.CostEstimate(flops=flops, bytes_accessed=moved, transcendentals=exps)


def limit(mib):
    return pltpu.CompilerParams(vmem_limit_bytes=mib << 20)


def tile_spec(every, m):
    return pl.BlockSpec(every.shape[:2] + (1,) + every.shape[3:], lambda *_: (0, 0, m, 0, 0), pipeline_mode=pl.Buffered(1))


def tile_of(ref):
    return ref[...].reshape(D, D)


def attend_kernel(qb, q_ref, k_ref, v_ref, o_ref, l_ref):
    rows = q_ref.shape[0]
    lane = lax.broadcasted_iota(jnp.int32, (qb, 128), 1)
    pair = pl.program_id(0)

    @pl.when(pair == 0)
    def _():
        l_ref[...] = jnp.zeros_like(l_ref)

    def step(i, carry):
        at = pl.ds(pl.multiple_of(i * qb, qb), qb)
        q = q_ref[at, :]
        outs = []
        low = l_ref[at, :]
        for h in range(2):
            own = (lane < HD) if h == 0 else (lane >= HD)
            s = nt(jnp.where(own, q, jnp.zeros_like(q)), k_ref[...])
            m = jnp.max(s, axis=1, keepdims=True)
            e = jnp.exp(s - m)
            t = jnp.sum(e, axis=1, keepdims=True)
            outs.append(nn(e.astype(bf16), v_ref[...]) * (1.0 / t))
            low = jnp.where(lane == 2 * pair + h, m + jnp.log(t), low)
        o_ref[at, :] = jnp.where(lane < HD, outs[0], outs[1]).astype(bf16)
        l_ref[at, :] = low
        return carry

    lax.fori_loop(0, rows // qb, step, 0)


def attend(q, k, v, qb=256):
    rows, total = q.shape[0], k.shape[0]
    qb = min(qb, rows)
    pair_q = pl.BlockSpec((rows, 128), lambda p: (0, p))
    pair_k = pl.BlockSpec((total, 128), lambda p: (0, p))
    return pl.pallas_call(
        functools.partial(attend_kernel, qb),
        grid=(HEADS // 2,),
        in_specs=[pair_q, pair_k, pair_k],
        out_specs=[pair_q, pl.BlockSpec((rows, 128), lambda p: (0, 0))],
        out_shape=[jax.ShapeDtypeStruct((rows, D), bf16), jax.ShapeDtypeStruct((rows, 128), f32)],
        compiler_params=limit(48),
        cost_estimate=cost(16 * rows * total * D, 8 * total * D, HEADS * rows * total),
        name="attend",
    )(q, k, v)


def attend_back_kernel(qb, q_ref, k_ref, v_ref, o_ref, g_ref, l_ref, dq_ref, dk_ref, dv_ref, dk_acc, dv_acc):
    rows = q_ref.shape[0]
    lane = lax.broadcasted_iota(jnp.int32, (qb, 128), 1)
    pair = pl.program_id(0)
    dk_acc[...] = jnp.zeros_like(dk_acc)
    dv_acc[...] = jnp.zeros_like(dv_acc)

    def step(i, carry):
        at = pl.ds(pl.multiple_of(i * qb, qb), qb)
        q = q_ref[at, :]
        g = g_ref[at, :]
        qt = q.astype(f32).T.astype(bf16)
        gt = g.astype(f32).T.astype(bf16)
        prod = o_ref[at, :].astype(f32) * g.astype(f32)
        low = l_ref[at, :]
        dqs = []
        for h in range(2):
            own = (lane < HD) if h == 0 else (lane >= HD)
            lse = jnp.sum(jnp.where(lane == 2 * pair + h, low, 0.0), axis=1, keepdims=True)
            delta = jnp.sum(jnp.where(own, prod, 0.0), axis=1, keepdims=True)
            s = nt(jnp.where(own, q, jnp.zeros_like(q)), k_ref[...])
            p = jnp.exp(s - lse)
            dp = nt(jnp.where(own, g, jnp.zeros_like(g)), v_ref[...])
            ds = (p * (dp - delta)).astype(bf16)
            part = pl.ds(h * HD, HD)
            dv_acc[part, :] += nn(gt[h * HD : (h + 1) * HD, :], p.astype(bf16))
            dk_acc[part, :] += nn(qt[h * HD : (h + 1) * HD, :], ds)
            dqs.append(nn(ds, k_ref[...]))
        dq_ref[at, :] = (jnp.where(lane < HD, dqs[0], dqs[1]) * (HD**-0.5)).astype(bf16)
        return carry

    lax.fori_loop(0, rows // qb, step, 0)
    dk_ref[...] = dk_acc[...].T.astype(bf16)
    dv_ref[...] = dv_acc[...].T.astype(bf16)


def attend_back(q, k, v, o, g, l, qb=512):
    rows, total = q.shape[0], k.shape[0]
    qb = min(qb, rows)
    pair_q = pl.BlockSpec((rows, 128), lambda p: (0, p))
    pair_k = pl.BlockSpec((total, 128), lambda p: (0, p))
    return pl.pallas_call(
        functools.partial(attend_back_kernel, qb),
        grid=(HEADS // 2,),
        in_specs=[pair_q, pair_k, pair_k, pair_q, pair_q, pl.BlockSpec((rows, 128), lambda p: (0, 0))],
        out_specs=[pair_q, pair_k, pair_k],
        out_shape=[
            jax.ShapeDtypeStruct((rows, D), bf16),
            jax.ShapeDtypeStruct((total, D), bf16),
            jax.ShapeDtypeStruct((total, D), bf16),
        ],
        scratch_shapes=[pltpu.VMEM((128, total), f32), pltpu.VMEM((128, total), f32)],
        compiler_params=limit(48),
        cost_estimate=cost(40 * rows * total * D, 16 * total * D, HEADS * rows * total),
        name="attend_back",
    )(q, k, v, o, g, l)


def fold_kernel(w0_ref, w1_ref, w2_ref, hi_ref, lo_ref, vec_ref, coef_ref, low_ref, lowt_ref, key_ref, query_ref):
    head = lax.broadcasted_iota(jnp.int32, (128, D), 0)
    column = lax.broadcasted_iota(jnp.int32, (128, D), 1)
    query = (nn(vec_ref[...].astype(bf16), tile_of(w0_ref))[0:1, :] + vec_ref[1:2, :]).astype(bf16)
    query_ref[...] = jnp.broadcast_to(query.astype(f32), query_ref.shape)
    spread = jnp.where(column // HD == head, query.astype(f32), 0.0).astype(bf16)
    key = nt(spread, tile_of(w1_ref)) * (HD**-0.5)
    key_ref[...] = key[:HEADS]
    key_hi = key.astype(bf16)
    key_lo = (key - key_hi.astype(f32)).astype(bf16)
    coef_ref[...] = nt(hi_ref[...], key_hi) + nt(lo_ref[...], key_hi) + nt(hi_ref[...], key_lo)
    value = tile_of(w2_ref)
    val = nn(hi_ref[...], value) + nn(lo_ref[...], value)
    row = lax.broadcasted_iota(jnp.int32, (TABLE, D), 0)
    val = jnp.where(row >= PIX * VARS, val + vec_ref[2:3, :], val)
    low_ref[...] = val.astype(bf16)
    lowt_ref[...] = val.T.astype(bf16)


def fold(every, hi, lo, vecs):
    return pl.pallas_call(
        fold_kernel,
        grid=(1,),
        in_specs=[*(tile_spec(every, m) for m in range(3)), once((TABLE, D)), once((TABLE, D)), once((8, D))],
        out_specs=[once(s) for s in ((TABLE, 128), (TABLE, D), (D, TABLE), (HEADS, D), (8, D))],
        out_shape=[
            jax.ShapeDtypeStruct((TABLE, 128), f32),
            jax.ShapeDtypeStruct((TABLE, D), bf16),
            jax.ShapeDtypeStruct((D, TABLE), bf16),
            jax.ShapeDtypeStruct((HEADS, D), f32),
            jax.ShapeDtypeStruct((8, D), f32),
        ],
        compiler_params=limit(60),
        cost_estimate=cost(6 * TABLE * D * D, 6 * D * D),
        name="fold",
    )(every, every, every, hi, lo, vecs)


def mix_probs(f, coef_ref, h):
    part = lambda k: coef_ref[k * VARS : (k + 1) * VARS, h : h + 1]
    s = part(PIX)
    for k in range(PIX):
        s = s + part(k) * f[k]
    e = jnp.exp(s - jnp.max(s, axis=0, keepdims=True))
    return e * (1.0 / jnp.sum(e, axis=0, keepdims=True))


def mix_kernel(f_ref, coef_ref, tt_ref, o_ref):
    f = [f_ref[0, k].astype(f32) for k in range(PIX)]

    def one(h):
        pa = mix_probs(f, coef_ref, h)
        pf = jnp.concatenate([pa * x for x in f] + [pa], axis=0).astype(bf16)
        return nn(tt_ref[h * HD : (h + 1) * HD, :], pf)

    for p in range(HEADS // 2):
        both = jnp.concatenate([one(2 * p), one(2 * p + 1)], axis=0)
        o_ref[:, p * 128 : (p + 1) * 128] = both.T.astype(bf16)


def mix(fields, coef, tt):
    nb, _, _, count = fields.shape
    return pl.pallas_call(
        mix_kernel,
        grid=(nb,),
        in_specs=[
            pl.BlockSpec((1, PIX, VARS, count), lambda b: (b, 0, 0, 0)),
            once((TABLE, 128)),
            once((D, TABLE)),
        ],
        out_specs=pl.BlockSpec((count, D), lambda b: (b, 0)),
        out_shape=jax.ShapeDtypeStruct((nb * count, D), bf16),
        compiler_params=limit(40),
        cost_estimate=cost(8 * nb * count * TABLE * D, 4 * nb * count * D, nb * count * VARS * HEADS),
        name="mix",
    )(fields, coef, tt)


def mix_back_kernel(side_ref, f_ref, coef_ref, t_ref, g_ref, rest_ref, mine_ref, other_ref, dt_ref, dc_ref):
    @pl.when(pl.program_id(0) == 0)
    def _():
        dc_ref[...] = jnp.zeros_like(dc_ref)
        dt_ref[...] = jnp.zeros_like(dt_ref)

    lane = lax.broadcasted_iota(jnp.int32, (VARS, 128), 1)
    f = [f_ref[0, k].astype(f32) for k in range(PIX)]
    for h in range(HEADS):
        pair = slice(h // 2 * 128, h // 2 * 128 + 128)
        own = (lane[:1] < HD) if h % 2 == 0 else (lane[:1] >= HD)
        pa = mix_probs(f, coef_ref, h)
        pf = jnp.concatenate([pa * x for x in f] + [pa], axis=0).astype(bf16)
        g = jnp.where(own, g_ref[:, pair], jnp.zeros((), bf16))
        dpf = nt(t_ref[:, pair], g)
        dpa = dpf[PIX * VARS :]
        for k in range(PIX):
            dpa = dpa + dpf[k * VARS : (k + 1) * VARS] * f[k]
        ds = pa * (dpa - jnp.sum(pa * dpa, axis=0, keepdims=True))
        for k in range(PIX + 1):
            w = ds * f[k] if k < PIX else ds
            dc_ref[k * VARS : (k + 1) * VARS, :] += jnp.where(lane == h, jnp.sum(w, axis=1, keepdims=True), 0.0)
        dt_ref[:, pair] += nn(pf, g)

    @pl.when(pl.program_id(0) == pl.num_programs(0) - 1)
    def _():
        dct = jnp.concatenate([dc_ref[...].T[:HEADS], jnp.zeros((HEADS, D // 2 - TABLE), f32)], axis=1)
        half = D // 2
        for at, left, right in (
            (0, dt_ref[:, :half], dt_ref[:, half:]),
            (TABLE, dct, jnp.zeros_like(dct)),
            (TABLE + HEADS, rest_ref[:, :half], rest_ref[:, half:]),
        ):
            rows = slice(at, at + left.shape[0])
            first = side_ref[0] == 0
            mine_ref[rows, :] = jnp.where(first, left, right)
            other_ref[rows, :] = jnp.where(first, right, left).astype(bf16)


def mix_back(side, fields, coef, t, g, rest):
    nb, _, _, count = fields.shape
    shape = (TABLE + HEADS + rest.shape[0], D // 2)
    whole = lambda s: pl.BlockSpec(s, lambda b: (0,) * len(s))
    return pl.pallas_call(
        mix_back_kernel,
        grid=(nb,),
        in_specs=[
            pl.BlockSpec(memory_space=pltpu.SMEM),
            pl.BlockSpec((1, PIX, VARS, count), lambda b: (b, 0, 0, 0)),
            once((TABLE, 128)),
            once((TABLE, D)),
            pl.BlockSpec((count, D), lambda b: (b, 0)),
            once(rest.shape),
        ],
        out_specs=[whole(shape), whole(shape)],
        out_shape=[jax.ShapeDtypeStruct(shape, f32), jax.ShapeDtypeStruct(shape, bf16)],
        scratch_shapes=[pltpu.VMEM((TABLE, D), f32), pltpu.VMEM((TABLE, 128), f32)],
        compiler_params=limit(40),
        cost_estimate=cost(16 * nb * count * TABLE * D, 4 * nb * count * D, nb * count * VARS * HEADS),
        name="mix_back",
    )(side, fields, coef, t, g, rest)


def front_kernel(m_ref, w3_ref, w4_ref, w5_ref, w6_ref, row_ref, col_ref, vec_ref, h_ref, a_ref, q_ref, k_ref, v_ref):
    per = row_ref.shape[1]
    h = nn(m_ref[...], tile_of(w3_ref))
    h = h + jnp.concatenate([col_ref[...] + row_ref[0, i : i + 1, :] for i in range(per)], axis=0)
    h_ref[...] = h
    center = h - jnp.mean(h, axis=-1, keepdims=True)
    inverse = lax.rsqrt(jnp.mean(center * center, axis=-1, keepdims=True) + norm_eps)
    a = (center * inverse * vec_ref[0:1, :] + vec_ref[1:2, :]).astype(bf16)
    a_ref[...] = a
    k_ref[...] = nn(a, tile_of(w5_ref)).astype(bf16)
    v_ref[...] = (nn(a, tile_of(w6_ref)) + vec_ref[3:4, :]).astype(bf16)

    @pl.when(pl.program_id(0) == 0)
    def _():
        q_ref[...] = ((nn(a, tile_of(w4_ref)) + vec_ref[2:3, :]) * (HD**-0.5)).astype(bf16)


def front(mixed, every, row, col, vecs, blocks):
    total = mixed.shape[0]
    count = total // blocks
    per = row.shape[0] // blocks
    block = pl.BlockSpec((count, D), lambda b: (b, 0))
    return pl.pallas_call(
        front_kernel,
        grid=(blocks,),
        in_specs=[
            block,
            *(tile_spec(every, m) for m in range(3, 7)),
            pl.BlockSpec((1, per, D), lambda b: (b, 0, 0)),
            once(col.shape),
            once(vecs.shape),
        ],
        out_specs=[block, block, pl.BlockSpec((count, D), lambda b: (0, 0)), block, block],
        out_shape=[
            jax.ShapeDtypeStruct((total, D), f32),
            jax.ShapeDtypeStruct((total, D), bf16),
            jax.ShapeDtypeStruct((count, D), bf16),
            jax.ShapeDtypeStruct((total, D), bf16),
            jax.ShapeDtypeStruct((total, D), bf16),
        ],
        compiler_params=limit(52),
        cost_estimate=cost(6 * total * D * D, 16 * total * D),
        name="front",
    )(mixed, *[every] * 4, row.reshape(blocks, per, D), col, vecs)


def norm_parts(values):
    center = values - jnp.mean(values, axis=-1, keepdims=True)
    inverse = lax.rsqrt(jnp.mean(center * center, axis=-1, keepdims=True) + norm_eps)
    return center * inverse, inverse


def norm_grad(grad, normed, inverse, gain):
    scaled = grad * gain
    return inverse * (
        scaled
        - jnp.mean(scaled, axis=-1, keepdims=True)
        - normed * jnp.mean(scaled * normed, axis=-1, keepdims=True)
    )


def column_sum(array):
    return jnp.sum(array, axis=0, keepdims=True)


def mlp_kernel(h0_ref, att_ref, wo_ref, one_ref, two_ref, vec_ref, head_ref, target_ref, factor_ref,
               act_ref, a2_ref, dh2_ref, du_ref, dh1_ref, dh1_low_ref, datt_ref, dhead_ref, sum_ref, loss_ref,
               h1, acc, grad2, slope):
    i = pl.program_id(0)
    folds = slope.shape[0]
    f = jnp.where(i < folds, i, 2 * folds - 1 - i)
    gain2, shift2, bias2, gain3, shift3 = [vec_ref[r : r + 1, :] for r in range(5)]

    @pl.when(i == 0)
    def _():
        h1[...] = h0_ref[...] + nn(att_ref[...], tile_of(wo_ref))
        normed, _ = norm_parts(h1[...])
        a2_ref[...] = (normed * gain2 + shift2).astype(bf16)
        acc[...] = h1[...] + bias2
        sum_ref[...] = jnp.zeros_like(sum_ref)

    @pl.when(i < folds)
    def _():
        u = nn(a2_ref[...], tile_of(one_ref)) + vec_ref[pl.ds(8 + f, 1), :]
        phi = 0.5 * (1.0 + lax.erf(u * 0.7071067811865476))
        slope[f] = phi + u * jnp.exp(-0.5 * u * u) * 0.3989422804014327
        act = (u * phi).astype(bf16)
        act_ref[...] = act
        acc[...] += nn(act, tile_of(two_ref))

    @pl.when(i == folds - 1)
    def _():
        normed, inverse = norm_parts(acc[...])
        z = (normed * gain3 + shift3).astype(bf16)
        error = nt(z, head_ref[...]) - target_ref[...]
        weighted = factor_ref[...] * error
        loss_ref[...] = jnp.broadcast_to(jnp.sum(column_sum(weighted * error), axis=1, keepdims=True), loss_ref.shape)
        dpred = (2.0 * weighted).astype(bf16)
        dhead_ref[...] = lax.dot_general(dpred, z, (((0,), (0,)), ((), ())), preferred_element_type=f32)
        dz = nn(dpred, head_ref[...])
        sum_ref[1:2, :] = column_sum(dz * normed)
        sum_ref[2:3, :] = column_sum(dz)
        grad = norm_grad(dz, normed, inverse, gain3)
        sum_ref[0:1, :] = column_sum(grad)
        grad2[...] = grad
        dh2_ref[...] = grad.astype(bf16)
        acc[...] = jnp.zeros_like(acc)

    @pl.when(i >= folds)
    def _():
        du = nt(dh2_ref[...], tile_of(two_ref)) * slope[f]
        sum_ref[pl.ds(6 + f, 1), :] = column_sum(du)
        low = du.astype(bf16)
        du_ref[...] = low
        acc[...] += nt(low, tile_of(one_ref))

    @pl.when(i == 2 * folds - 1)
    def _():
        normed, inverse = norm_parts(h1[...])
        grad = acc[...]
        sum_ref[3:4, :] = column_sum(grad * normed)
        sum_ref[4:5, :] = column_sum(grad)
        grad = grad2[...] + norm_grad(grad, normed, inverse, gain2)
        dh1_ref[...] = grad
        low = grad.astype(bf16)
        dh1_low_ref[...] = low
        datt_ref[...] = nt(low, tile_of(wo_ref)).astype(bf16)


def mlp(hidden0, attended, first, second, vecs, head, targets, factor):
    count, width = targets.shape
    folds = FF // D
    fold = lambda i: jnp.where(i < folds, i, 2 * folds - 1 - i)
    tile = lambda base: pl.BlockSpec(
        second.shape[:2] + (1,) + second.shape[3:], lambda i: (0, 0, base + fold(i), 0, 0)
    )
    fixed = lambda s: pl.BlockSpec(s, lambda i: (0,) * len(s))
    state = (count, D)
    return pl.pallas_call(
        mlp_kernel,
        grid=(2 * folds,),
        in_specs=[
            once(state), once(state), tile_spec(first, 7), tile(0), tile(folds), once(vecs.shape), once(head.shape),
            once(targets.shape), once(factor.shape),
        ],
        out_specs=[
            pl.BlockSpec(state, lambda i: (0, jnp.minimum(i, folds - 1))),
            fixed(state),
            fixed(state),
            pl.BlockSpec(state, lambda i: (0, jnp.minimum(2 * folds - 1 - i, folds - 1))),
            fixed(state),
            fixed(state),
            fixed(state),
            fixed(head.shape),
            fixed((16, D)),
            fixed((8, 128)),
        ],
        out_shape=[
            jax.ShapeDtypeStruct((count, FF), bf16),
            jax.ShapeDtypeStruct(state, bf16),
            jax.ShapeDtypeStruct(state, bf16),
            jax.ShapeDtypeStruct((count, FF), bf16),
            jax.ShapeDtypeStruct(state, f32),
            jax.ShapeDtypeStruct(state, bf16),
            jax.ShapeDtypeStruct(state, bf16),
            jax.ShapeDtypeStruct(head.shape, f32),
            jax.ShapeDtypeStruct((16, D), f32),
            jax.ShapeDtypeStruct((8, 128), f32),
        ],
        scratch_shapes=[
            pltpu.VMEM(state, f32), pltpu.VMEM(state, f32), pltpu.VMEM(state, f32), pltpu.VMEM((folds,) + state, f32)
        ],
        compiler_params=limit(60),
        cost_estimate=cost(8 * count * D * FF, 20 * D * FF, 2 * count * FF),
        name="mlp",
    )(hidden0, attended, first, second, second, vecs, head, targets, factor)


def back_kernel(dq_ref, dk_ref, dv_ref, h_ref, dh_ref, w3_ref, w4_ref, w5_ref, w6_ref, vec_ref, g_ref, gm_ref, sum_ref, acc):
    first = pl.program_id(0) == 0
    acc[...] = nt(dk_ref[...], tile_of(w5_ref)) + nt(dv_ref[...], tile_of(w6_ref))

    @pl.when(first)
    def _():
        sum_ref[...] = jnp.zeros_like(sum_ref)
        acc[...] += nt(dq_ref[...], tile_of(w4_ref))
        sum_ref[4:5, :] = jnp.sum(dq_ref[...].astype(f32), axis=0, keepdims=True)

    h = h_ref[...]
    center = h - jnp.mean(h, axis=-1, keepdims=True)
    inverse = lax.rsqrt(jnp.mean(center * center, axis=-1, keepdims=True) + norm_eps)
    normed = center * inverse
    grad = acc[...]
    sum_ref[1:2, :] += jnp.sum(grad * normed, axis=0, keepdims=True)
    sum_ref[2:3, :] += jnp.sum(grad, axis=0, keepdims=True)
    sum_ref[3:4, :] += jnp.sum(dv_ref[...].astype(f32), axis=0, keepdims=True)
    scaled = grad * vec_ref[0:1, :]
    out = inverse * (
        scaled
        - jnp.mean(scaled, axis=-1, keepdims=True)
        - normed * jnp.mean(scaled * normed, axis=-1, keepdims=True)
    )
    acc[...] = out

    @pl.when(first)
    def _():
        acc[...] += dh_ref[...]

    out = acc[...]
    sum_ref[0:1, :] += jnp.sum(out, axis=0, keepdims=True)
    low = out.astype(bf16)
    g_ref[...] = low
    gm_ref[...] = nt(low, tile_of(w3_ref)).astype(bf16)


def back(dq, dk, dv, h, dh, every, vecs, blocks):
    total = dk.shape[0]
    count = total // blocks
    block = pl.BlockSpec((count, D), lambda b: (b, 0))
    return pl.pallas_call(
        back_kernel,
        grid=(blocks,),
        in_specs=[
            once((count, D)),
            block,
            block,
            block,
            once((count, D)),
            *(tile_spec(every, m) for m in range(3, 7)),
            once(vecs.shape),
        ],
        out_specs=[block, block, pl.BlockSpec((8, D), lambda b: (0, 0))],
        out_shape=[
            jax.ShapeDtypeStruct((total, D), bf16),
            jax.ShapeDtypeStruct((total, D), bf16),
            jax.ShapeDtypeStruct((8, D), f32),
        ],
        scratch_shapes=[pltpu.VMEM((count, D), f32)],
        compiler_params=limit(52),
        cost_estimate=cost(7 * total * D * D, 16 * total * D),
        name="back",
    )(dq, dk, dv, h, dh, *[every] * 4, vecs)


def choose_kernel(first, slot_ref, p_ref, wait_ref, out_ref):
    for m in range(out_ref.shape[0]):
        out_ref[m] = p_ref[slot_ref[first + m]]


def choose(slot_of, pieces, first, count, wait):
    shape = (count,) + pieces.shape[1:]
    whole = lambda s: pl.BlockSpec(s, lambda i, at: (0, 0, 0))
    return pl.pallas_call(
        functools.partial(choose_kernel, first),
        grid_spec=pltpu.PrefetchScalarGridSpec(
            num_scalar_prefetch=1,
            grid=(1,),
            in_specs=[whole(pieces.shape), pl.BlockSpec(memory_space=pltpu.HBM)],
            out_specs=whole(shape),
        ),
        out_shape=jax.ShapeDtypeStruct(shape, pieces.dtype),
        compiler_params=limit(60),
        cost_estimate=cost(0, 4 * pieces.size),
        name="choose",
    )(slot_of, pieces, wait)


def finish_kernel(plan, slot_ref, *refs):
    ins, out, square = refs[:-2], refs[-2], refs[-1]
    half = out.shape[2]
    for m in range(3):
        out[slot_ref[m]] = jnp.zeros_like(out[0])
    total = jnp.zeros(out.shape[1:], f32)
    ins = list(ins)
    for per, tiles in plan:
        job, ins = ins[:per], ins[per:]
        for m, index, col in tiles:
            parts = [r[index, :, col * half : (col + 1) * half].astype(f32) for r in job]
            value = sum(parts[1:], parts[0])
            out[slot_ref[m]] = value.astype(out.dtype)
            total = total + value * value
    square[...] = jnp.sum(total.reshape(total.shape[0] // 8, 8, half), axis=0)


def finish(slot_of, plan, jobs):
    arrays = [a for job in jobs for a in job]
    plan = tuple((len(job), tiles) for job, tiles in zip(jobs, plan))
    rows, half = arrays[0].shape[1], D // 2
    whole = lambda s: pl.BlockSpec(s, lambda i, at: (0,) * len(s))
    n = slot_of.shape[0]
    return pl.pallas_call(
        functools.partial(finish_kernel, plan),
        grid_spec=pltpu.PrefetchScalarGridSpec(
            num_scalar_prefetch=1,
            grid=(1,),
            in_specs=[whole(a.shape) for a in arrays],
            out_specs=[whole((n, rows, half)), whole((8, half))],
        ),
        out_shape=[jax.ShapeDtypeStruct((n, rows, half), bf16), jax.ShapeDtypeStruct((8, half), f32)],
        compiler_params=limit(48),
        cost_estimate=cost(0, 3 * 4 * n * rows * half),
        name="finish",
    )(slot_of, *arrays)


beta_one = 0.9
beta_two = 0.95
rate_tiles = 0.01
rate_vectors = 0.1
decay_weight = 1e-05
adam_eps = 1e-08
STEP = 10
clip_norm = 0.02


def adam_update(weight, grad, first, second, rate):
    first = beta_one * first + (1.0 - beta_one) * grad
    second = beta_two * second + (1.0 - beta_two) * grad * grad
    first_hat = first / (1.0 - beta_one**STEP)
    second_hat = second / (1.0 - beta_two**STEP)
    weight = weight - rate * (first_hat / (jnp.sqrt(second_hat) + adam_eps) + decay_weight * weight)
    return (weight, first, second)


def tail_kernel(square_ref, w0_ref, w1_ref, w2_ref, hi_ref, lo_ref, gram_ref, key_ref, query_ref, vec_ref, late_ref,
                p_ref, m_ref, v_ref, clip_ref, gkey_ref, agg_ref, p_new, m_new, v_new, ge, extra):
    head = lax.broadcasted_iota(jnp.int32, (HEADS, D), 0)
    column = lax.broadcasted_iota(jnp.int32, (HEADS, D), 1)

    def parts(a):
        high = a.astype(bf16)
        return high, (a - high.astype(f32)).astype(bf16)

    def tn(a, b):
        return lax.dot_general(a, b, (((0,), (0,)), ((), ())), preferred_element_type=f32)

    offset = PIX * VARS
    fold_ref, head_ref = late_ref.at[0:TABLE, :], late_ref.at[TABLE + 40 : TABLE + 40 + offset, :]
    coef_hi, coef_lo = parts(late_ref[TABLE : TABLE + HEADS, 0:256][:, :TABLE])
    grad_key = (nn(coef_hi, hi_ref[...]) + nn(coef_hi, lo_ref[...]) + nn(coef_lo, hi_ref[...])) * (HD**-0.5)
    gkey_ref[...] = grad_key
    key_hi, key_lo = parts(grad_key)
    by_head = nn(key_hi, tile_of(w1_ref)) + nn(key_lo, tile_of(w1_ref))
    agg = jnp.sum(jnp.where(column // HD == head, by_head, 0.0), axis=0, keepdims=True)
    agg_ref[...] = jnp.broadcast_to(agg, agg_ref.shape)
    agg_hi, agg_lo = parts(jnp.broadcast_to(agg, (8, D)))
    by_query = (nt(agg_hi, tile_of(w0_ref)) + nt(agg_lo, tile_of(w0_ref)))[0:1]
    fold_hi, fold_lo = parts(fold_ref[...])
    fold_key_hi, fold_key_lo = parts(key_ref[...])
    ge[...] = (
        nt(fold_hi, tile_of(w2_ref)) + nt(fold_lo, tile_of(w2_ref))
        + tn(coef_hi, fold_key_hi) + tn(coef_hi, fold_key_lo) + tn(coef_lo, fold_key_hi)
    )
    rest = late_ref[TABLE + HEADS : TABLE + HEADS + 24, :]
    order = [
        by_query, rest[5:6], rest[0:1], agg, jnp.sum(fold_ref[offset:, :], axis=0, keepdims=True), rest[0:1],
        rest[1:2], rest[2:3], rest[4:5], rest[3:4], rest[11:12], rest[12:13], rest[8:9], rest[9:10], rest[10:11],
    ]
    for i, r in enumerate(order):
        extra[i : i + 1, :] = r
    extra[15:19, :] = rest[14:18]
    gram_hi, gram_lo = parts(gram_ref[...])
    through = nn(gram_hi, fold_hi) + nn(gram_hi, fold_lo) + nn(gram_lo, fold_hi)
    total = jnp.sum(through * fold_ref[...], axis=0, keepdims=True)
    total += jnp.sum(ge[...] * ge[...], axis=0, keepdims=True)
    bias = ge[offset:, :]
    total += jnp.sum(bias * bias, axis=0, keepdims=True)
    total += jnp.sum(head_ref[...] * head_ref[...], axis=0, keepdims=True)
    total += jnp.sum(extra[0:19, :] * extra[0:19, :], axis=0, keepdims=True)
    vq = vec_ref[0:1, :].astype(bf16).astype(f32)
    total = jnp.sum(total, axis=1, keepdims=True)
    total += jnp.sum(vq * vq, axis=1, keepdims=True) * jnp.sum(agg * agg, axis=1, keepdims=True)
    query = query_ref[0:1, :]
    per_head = jnp.sum(jnp.where(column // HD == head, query * query, 0.0), axis=1, keepdims=True)
    total += jnp.sum(jnp.sum(grad_key * grad_key, axis=1, keepdims=True) * per_head, axis=0, keepdims=True)
    norm = jnp.sqrt(total + square_ref[0])
    clip = jnp.minimum(1.0, clip_norm / (norm + 1e-06))
    lane = lax.broadcasted_iota(jnp.int32, (8, 128), 1)
    clip_ref[...] = jnp.where(lane == 0, clip, norm)

    def update(rows, grad):
        p_new[rows, :], m_new[rows, :], v_new[rows, :] = adam_update(
            p_ref[rows, :], grad * clip, m_ref[rows, :], v_ref[rows, :], rate_vectors
        )

    for k in range(PIX):
        for v in range(VARS):
            extra_row = 32 + v * PIX + k
            extra[extra_row : extra_row + 1, :] = ge[k * VARS + v : k * VARS + v + 1, :]
    update(pl.ds(0, offset), extra[32 : 32 + offset, :])
    update(pl.ds(offset, VARS), bias)
    update(pl.ds(offset + VARS, VARS), bias)
    update(pl.ds(offset + 2 * VARS, offset), head_ref[...])
    update(pl.ds(2 * offset + 2 * VARS, 19), extra[0:19, :])


def tail(square, every, hi, lo, gram, key, query, vecs, late, w, m, v):
    vmem = pl.BlockSpec(memory_space=pltpu.VMEM)
    arrays = (hi, lo, gram, key, query, vecs, late, w, m, v)
    return pl.pallas_call(
        tail_kernel,
        grid=(1,),
        in_specs=[pl.BlockSpec(memory_space=pltpu.SMEM), *(tile_spec(every, m) for m in range(3))]
        + [once(a.shape) for a in arrays],
        out_specs=[once(s) for s in ((8, 128), (HEADS, D), (8, D), w.shape, w.shape, w.shape)],
        out_shape=[
            jax.ShapeDtypeStruct(s, f32) for s in ((8, 128), (HEADS, D), (8, D), w.shape, w.shape, w.shape)
        ],
        scratch_shapes=[pltpu.VMEM((TABLE, D), f32), pltpu.VMEM((32 + PIX * VARS, D), f32)],
        compiler_params=limit(36),
        cost_estimate=cost(8 * TABLE * D * D, 28 * w.size),
        name="tail",
    )(square, every, every, every, *arrays)


PROWS = 32
PCOLS = 64
GROUPS = 5
HIGHEST = lax.Precision.HIGHEST
clip_norm = 0.02
SCALE = HD**-0.5


def position_parts():
    quarter = D // 4
    omega = jnp.exp(-math.log(10000.0) * jnp.arange(quarter).astype(f32) / quarter)
    row = jnp.arange(PROWS).astype(f32)[:, None] * omega[None, :]
    col = jnp.arange(PCOLS).astype(f32)[:, None] * omega[None, :]
    zero_row = jnp.zeros((PROWS, D // 2), f32)
    zero_col = jnp.zeros((PCOLS, D // 2), f32)
    row_part = jnp.concatenate([jnp.sin(row), jnp.cos(row), zero_row], axis=1)
    col_part = jnp.concatenate([zero_col, jnp.sin(col), jnp.cos(col)], axis=1)
    return row_part, col_part


def latitude_table(start, count):
    index = start + jnp.arange(count)
    inner = jnp.arange(PIX) // 2
    lat_rows = 2 * (index // PCOLS)[:, None] + inner[None, :]
    total_rows = 2 * PROWS
    angle = (lat_rows.astype(f32) + 0.5) * (math.pi / total_rows) - math.pi / 2
    every = (jnp.arange(total_rows).astype(f32) + 0.5) * (math.pi / total_rows) - math.pi / 2
    weight = jnp.cos(angle) / jnp.mean(jnp.cos(every))
    return jnp.tile(weight, (1, VARS))


def tn(left, right):
    return lax.dot_general(left, right, (((0,), (0,)), ((), ())), preferred_element_type=f32)


def split_low(values):
    high = lax.reduce_precision(values, 8, 7)
    return high.astype(bf16), (values - high).astype(bf16)


def swap(array, bit):
    n = lax.axis_size("dp")
    return lax.ppermute(array, "dp", [(i, i ^ bit) for i in range(n)])


def shift(array, step):
    n = lax.axis_size("blk")
    return lax.ppermute(array, "blk", [(i, (i + step) % n) for i in range(n)])


def dp_bits():
    return [1 << i for i in range(lax.axis_size("dp").bit_length() - 1)]


def after(array, *others):
    return lax.optimization_barrier((array, *others))[0]


def pick(array, axis, index):
    return lax.dynamic_index_in_dim(array, index, axis, False)


def halves(array, side):
    half = array.shape[-1] // 2
    left, right = array[..., :half], array[..., half:]
    return jnp.where(side == 0, left, right), jnp.where(side == 0, right, left)


def sum_small(values):
    n_dp, blocks = lax.axis_size("dp"), lax.axis_size("blk")
    me = lax.axis_index("blk") * n_dp + lax.axis_index("dp")
    width = -(-n_dp * blocks // 128) * 128
    array = jnp.where(jnp.arange(width)[None, :] == me, values[:, None], 0.0)
    array = sum([shift(array, k) for k in range(1, blocks)], array)
    array = sum([swap(array, 2 * mask) for mask in range(1, n_dp // 2)], array)
    return jnp.sum(array + swap(array, 1), axis=1)


def gather_blocks(array):
    n = lax.axis_size("blk")
    return jnp.stack([array] + [shift(array, k) for k in range(1, n)])


def gather(pieces):
    blocks, n_dp = lax.axis_size("blk"), lax.axis_size("dp")
    return lax.all_gather(pieces, ("blk", "dp"), axis=0).reshape((blocks, n_dp) + pieces.shape)


class SplitSum:
    def __init__(self, cur, order, low=True):
        self.blocks = lax.axis_size("blk")
        self.left = list(reversed(dp_bits()[1:]))
        rows = cur.shape[1] // (self.blocks << len(self.left))
        self.cur = cur.reshape((cur.shape[0], self.blocks) + (2,) * len(self.left) + (rows,) + cur.shape[2:])
        self.order = list(order)
        self.type = bf16 if low else f32
        self.got = []

    @classmethod
    def joined(cls, jobs):
        job = cls.__new__(cls)
        for other in jobs:
            other.take()
        job.blocks, job.type, job.got = jobs[0].blocks, jobs[0].type, []
        job.cur = jnp.concatenate([other.cur for other in jobs], axis=0)
        return job

    def take(self):
        for got in self.got:
            self.cur = self.cur + got.astype(f32)
        self.got = []

    def send(self):
        self.take()
        bit = self.order.pop(0)
        axis = 2 + self.left.index(bit)
        mine = (lax.axis_index("dp") // bit) % 2
        sent = pick(self.cur, axis, 1 - mine).astype(self.type)
        self.cur = pick(self.cur, axis, mine)
        self.left.remove(bit)
        self.got = [swap(sent, bit)]
        return sent

    def send_all(self):
        self.take()
        order, n, at = self.order, 1 << len(self.left), 2
        own = lax.axis_index("dp") // 2
        cur = self.cur.reshape(self.cur.shape[:2] + (n,) + self.cur.shape[2 + len(self.left) :])
        sent = [pick(cur, at, own ^ mask).astype(self.type) for mask in range(1, n)]
        self.cur, self.order, self.left = pick(cur, at, own), [], []
        self.got = [swap(a, 2 * (i + 1)) for i, a in enumerate(sent)]
        return sent

    def send_blocks(self):
        self.take()
        blk = lax.axis_index("blk")
        sent = [pick(self.cur, 1, (blk + k) % self.blocks).astype(self.type) for k in range(1, self.blocks)]
        self.cur = pick(self.cur, 1, blk)
        self.got = [shift(a, k + 1) for k, a in enumerate(sent)]
        return sent

    def parts(self):
        return [self.cur, *self.got]

    def end(self):
        for got in self.got:
            self.cur = self.cur + got.astype(f32)
        self.got = []
        return self.cur


class SumRows:
    def __init__(self, mine, other):
        self.rows = mine.shape[0]
        self.side = lax.axis_index("dp") % 2
        self.job = SplitSum((mine + swap(other, 1).astype(f32))[None], dp_bits()[1:])
        self.steps = [self.job.send_all, self.job.send_blocks, self.widen_blocks, self.widen, self.close]

    def step(self):
        return self.steps.pop(0)()

    def widen_blocks(self):
        part = self.job.end()[0].astype(bf16)
        n, blk = lax.axis_size("blk"), lax.axis_index("blk")
        cur = gather_blocks(part)
        self.cur = jnp.stack([pick(cur, 0, (blk - z + n) % n) for z in range(n)])

    def widen(self):
        n, own = lax.axis_size("dp") // 2, lax.axis_index("dp") // 2
        every = jnp.stack([self.cur] + [swap(self.cur, 2 * mask) for mask in range(1, n)])
        self.cur = jnp.stack([pick(every, 0, own ^ i) for i in range(n)], axis=1).reshape(self.rows, -1)

    def close(self):
        cur, got = self.cur, swap(self.cur, 1)
        whole = jnp.where(self.side == 0, jnp.concatenate([cur, got], 1), jnp.concatenate([got, cur], 1))
        return whole.astype(f32)

    def end(self):
        while len(self.steps) > 1:
            self.step()
        return self.step()


def shards(fields, targets, lead_time, pixel_mask, group_id, slot_of, tiles, tiles_m, tiles_v, vectors, vec_m, vec_v):
    _, count, _ = fields.shape
    blocks, n_dp = lax.axis_size("blk"), lax.axis_size("dp")
    total = count * blocks
    folds = FF // D
    dp, blk = lax.axis_index("dp"), lax.axis_index("blk")
    side = dp % 2
    start = blk * count
    others = dp_bits()[1:]
    first_order, second_order = tuple(others), tuple(reversed(others))
    slots, tall, _ = tiles.shape
    n_tiles = slots * n_dp
    rows = 2 * tall // n_dp
    half = D // 2
    fine = tall // n_dp % 16 == 0

    mask_float = pixel_mask[0].astype(f32)
    var_local = jnp.sum(jnp.sum(mask_float, axis=0).reshape(VARS, PIX), axis=1)
    group_hot = (group_id[0] == jnp.arange(GROUPS)).astype(f32)
    counted = sum_small(jnp.pad(jnp.concatenate([var_local, group_hot]), (0, 64 - VARS - GROUPS)))
    field_t = fields[0].astype(bf16).reshape(count, VARS, PIX).transpose(2, 1, 0)
    field_all = gather_blocks(field_t)

    if fine:
        low_rows = tall // n_dp
        pieces = tiles.astype(bf16).reshape(slots, n_dp, low_rows, D)
        pieces = lax.all_to_all(pieces, "dp", 1, 0, tiled=True).reshape(n_tiles, low_rows, D)
        first = gather(choose(slot_of, pieces, 0, 8, field_all))
    else:
        slots_low = lax.all_gather(tiles.astype(bf16), "blk", axis=1, tiled=True)
        slots_low = lax.all_gather(slots_low, "dp", axis=0, tiled=True)
        weights = [pick(slots_low, 0, slot_of[m]) for m in range(n_tiles)]
        first = jnp.stack(weights[:8])[None, None]
        second = jnp.stack(weights[8:])[None, None]

    var_total, group_total = counted[:VARS], counted[VARS : VARS + GROUPS] / blocks
    sample_weight = jnp.sum(group_total) / (GROUPS * jnp.sum(group_hot * group_total))
    count_pixels = VARS * jnp.repeat(var_total, PIX)
    factor = sample_weight * mask_float * latitude_table(start, count) / count_pixels

    offset = VARS * PIX
    embed_weight = vectors[:offset].reshape(VARS, PIX, D).transpose(1, 0, 2).reshape(offset, D)
    embed_bias = vectors[offset : offset + VARS] + vectors[offset + VARS : offset + 2 * VARS]
    embed = jnp.concatenate([embed_weight, embed_bias], axis=0)
    head_low = vectors[offset + 2 * VARS : 2 * offset + 2 * VARS].astype(bf16)
    extras = vectors[2 * offset + 2 * VARS :]
    gram = lax.dot_general(embed, embed, NT, precision=HIGHEST, preferred_element_type=f32)
    embed_hi, embed_lo = split_low(embed)

    fold_vecs = jnp.concatenate([extras[0:1], extras[3:5], jnp.zeros((5, D), f32)], axis=0)
    fold_vecs = after(fold_vecs, counted, field_all[:, 0, :8, :128])
    coef, fold_low, fold_low_t, fold_key, query_f = fold(first, embed_hi, embed_lo, fold_vecs)
    if fine:
        second = gather(choose(slot_of, pieces, 8, 8, first))
    mixed = mix(field_all, coef, fold_low_t)

    row_part, col_part = position_parts()
    row_part = row_part.reshape(blocks, PROWS // blocks, D)
    row_here = jnp.concatenate([pick(row_part, 0, (blk - k + blocks) % blocks) for k in range(blocks)], axis=0)
    lead_row = extras[5] + lead_time[0] * extras[1] + extras[2]
    vecs = jnp.concatenate([extras[6:10], jnp.zeros((4, D), f32)], axis=0)
    hidden0, normed1_low, query_blk, key_all, value_all = front(
        mixed, first, row_here + lead_row, col_part, vecs, blocks
    )
    own1_low = normed1_low[:count]
    attended_low, log_total = attend(query_blk, key_all, value_all)

    mlp_vecs = jnp.concatenate([extras[10:15], jnp.zeros((3, D), f32), extras[15 : 15 + folds], jnp.zeros((4, D), f32)], axis=0)
    (activ_low, normed2_low, grad_h2_low, grad_pre_low, grad_h1, grad_h1_low, grad_attended, grad_head, mlp_sums,
     loss_local) = mlp(hidden0, attended_low, first, second, mlp_vecs, head_low, targets[0], factor)
    loss_local = loss_local[0, 0]

    def weight_grads(left, mine, other):
        sent = tn(left, other).astype(bf16)
        return tn(left, mine), swap(sent, 1), sent

    both = lambda parts: parts[0] + parts[1].astype(f32)
    if fine:
        two_parts = weight_grads(activ_low, *halves(grad_h2_low, side))
        left, right = [
            jnp.concatenate([grad_pre_low[:, f * D + s * half : f * D + (s + 1) * half] for f in range(folds)], axis=1)
            for s in range(2)
        ]
        one_parts = weight_grads(normed2_low, jnp.where(side == 0, left, right), jnp.where(side == 0, right, left))
        two_job = SplitSum(both(two_parts).reshape(folds, D, half), first_order)
        one_job = SplitSum(both(one_parts)[None], second_order)
    early = jnp.concatenate([mlp_sums, grad_head], axis=0)
    if fine:
        grad_attended = after(grad_attended, two_job.send(), one_job.send(), early)
    grad_query, grad_keys, grad_values = attend_back(query_blk, key_all, value_all, attended_low, grad_attended, log_total)
    if fine:
        sent = [two_job.send(), one_job.send()]
        grad_query, grad_keys, grad_values, *_ = lax.optimization_barrier((grad_query, grad_keys, grad_values, *sent))
        query_parts = weight_grads(own1_low, *halves(grad_query, side))
        out_parts = weight_grads(attended_low, *halves(grad_h1_low, side))
        key_parts = weight_grads(normed1_low, *halves(grad_keys, side))
        value_parts = weight_grads(normed1_low, *halves(grad_values, side))
        pair_job = SplitSum(jnp.stack([both(key_parts), both(value_parts)]), second_order)
        end_job = SplitSum(jnp.stack([both(query_parts), both(out_parts)]), first_order)
        grad_query = after(grad_query, pair_job.send(), end_job.send())
    grad_h0_low, grad_mixed, sums = back(grad_query, grad_keys, grad_values, hidden0, grad_h1, first, vecs, blocks)
    sums = jnp.where(jnp.arange(8)[:, None] == 5, sums[0] * lead_time[0], sums)
    step = 16 * (n_dp // 2) * blocks
    below = sums.shape[0] + early.shape[0]
    rest = jnp.concatenate([sums, early, jnp.zeros((-(TABLE + HEADS + below) % step, D), f32)], axis=0)
    if fine:
        sent = [pair_job.send(), end_job.send(), *two_job.send_blocks(), *one_job.send_blocks(), rest]
        grad_h0_low, grad_mixed, *_, rest = lax.optimization_barrier((grad_h0_low, grad_mixed, *sent))
        agg_parts = weight_grads(mixed, *halves(grad_h0_low, side))
        agg_job = SplitSum(both(agg_parts)[None], first_order)
        grad_mixed = after(grad_mixed, agg_parts[2])
    late_mine, late_other = mix_back(side.reshape(1), field_all, coef, fold_low, grad_mixed, rest)
    if fine:
        late_mine, late_other, *_ = lax.optimization_barrier((late_mine, late_other, *agg_job.send_all()))
    late_job = SumRows(late_mine, late_other)
    if fine:
        edge_job = SplitSum.joined([end_job, pair_job])
        sent = [*edge_job.send_blocks(), two_job.end(), one_job.end()]
        late_job.step()
        late_job.job.cur = after(late_job.job.cur, *sent)
        agg_job.send_blocks()
        plan = (
            [(12 + f, f, 0) for f in range(folds)],
            [(8 + f, 0, f) for f in range(folds)],
            [(m, i, 0) for i, m in enumerate((4, 7, 5, 6))],
            [(3, 0, 0)],
        )
        by_slot, square = finish(slot_of, plan, [j.parts() for j in (two_job, one_job, edge_job, agg_job)])
        part_square = jnp.sum(square)
        while len(late_job.steps) > 1:
            late_job.step()
        by_slot, late_job.cur = lax.optimization_barrier((by_slot, late_job.cur))
        by_slot = lax.all_to_all(by_slot, "dp", 0, 0, tiled=True).astype(f32)
        slot_grads = by_slot.reshape(n_dp // 2, 2, slots, rows, half).transpose(2, 0, 3, 1, 4).reshape(slots, tall, D)
    else:
        rest = [tn(mixed, grad_h0_low), tn(own1_low, grad_query), tn(normed1_low, grad_keys),
                tn(normed1_low, grad_values), tn(attended_low, grad_h1_low)]
        rest += [tn(normed2_low, grad_pre_low[:, f * D : (f + 1) * D]) for f in range(folds)]
        rest += [tn(activ_low[:, f * D : (f + 1) * D], grad_h2_low) for f in range(folds)]
        by_slot = jnp.zeros((n_tiles, D, D), f32)
        for m, grad in enumerate(rest):
            by_slot = lax.dynamic_update_index_in_dim(by_slot, grad, slot_of[m + 3], 0)
        slot_grads = lax.psum_scatter(by_slot, "dp", scatter_dimension=0, tiled=True)
        slot_grads = lax.psum_scatter(slot_grads, "blk", scatter_dimension=1, tiled=True)
        part_square = jnp.sum(slot_grads * slot_grads)
    late = late_job.end()
    numbers = sum_small(jnp.pad(jnp.stack([part_square, loss_local]), (0, 6)))
    loss = numbers[1]
    clips, grad_key, grad_agg, vectors_new, vec_m_new, vec_v_new = tail(
        numbers[:1], first, embed_hi, embed_lo, gram, fold_key, query_f, fold_vecs, late, vectors, vec_m, vec_v
    )
    clip, grad_norm = clips[0, 0], clips[0, 1]

    at_rows = blk * tall
    var_query_f = extras[0].astype(bf16).astype(f32)
    own_first = lax.dynamic_slice_in_dim(var_query_f, at_rows, tall, 0)[:, None] * grad_agg[0][None, :]
    own_key = lax.dynamic_slice_in_dim(grad_key, at_rows, tall, 1)
    own_second = jnp.repeat(own_key.T, HD, axis=1) * query_f[0][None, :]
    own_third = lax.dot_general(
        lax.dynamic_slice_in_dim(embed, at_rows, tall, 1), late[:TABLE], (((0,), (0,)), ((), ())),
        precision=HIGHEST, preferred_element_type=f32,
    )
    my_tiles = [jnp.sum(jnp.where(slot_of == dp * slots + t, jnp.arange(n_tiles), 0)) for t in range(slots)]
    shard_grads = jnp.stack(
        [
            jnp.where(m == 0, own_first, jnp.where(m == 1, own_second, jnp.where(m == 2, own_third, slot_grads[t])))
            for t, m in enumerate(my_tiles)
        ]
    )
    tiles_new, tiles_m_new, tiles_v_new = adam_update(tiles, shard_grads * clip, tiles_m, tiles_v, rate_tiles)
    return (loss, grad_norm, tiles_new, tiles_m_new, tiles_v_new, vectors_new, vec_m_new, vec_v_new)


def solution(mesh):
    tile = P("dp", "blk", None)
    placed = (tile, tile, P("dp"), tile, P("dp"), P(), tile, tile, tile, P(), P(), P())
    return jax.shard_map(
        shards,
        mesh=mesh,
        in_specs=placed,
        out_specs=(P(), P(), tile, tile, tile, P(), P(), P()),
        check_vma=False,
    )
```

```python
import functools
import math

import jax
import jax.numpy as jnp
from jax import lax
from jax.experimental import pallas as pl
from jax.experimental.pallas import tpu as pltpu
from jax.sharding import PartitionSpec as P

D = 1024
HEADS = 16
HD = 64
FF = 4096
VARS = 48
PIX = 4
TABLE = (PIX + 1) * VARS
norm_eps = 1e-05
f32 = jnp.float32
bf16 = jnp.bfloat16
NT = (((1,), (1,)), ((), ()))
NN = (((1,), (0,)), ((), ()))


def nt(a, b):
    return lax.dot_general(a, b, NT, preferred_element_type=f32)


def nn(a, b):
    return lax.dot_general(a, b, NN, preferred_element_type=f32)


def once(shape):
    zeros = (0,) * len(shape)
    return pl.BlockSpec(shape, lambda *_: zeros, pipeline_mode=pl.Buffered(1))


def cost(flops, moved, exps=0):
    return pl.CostEstimate(flops=flops, bytes_accessed=moved, transcendentals=exps)


def limit(mib):
    return pltpu.CompilerParams(vmem_limit_bytes=mib << 20)


def tile_spec(every, m):
    return pl.BlockSpec(every.shape[:2] + (1,) + every.shape[3:], lambda *_: (0, 0, m, 0, 0), pipeline_mode=pl.Buffered(1))


def tile_of(ref):
    return ref[...].reshape(D, D)


def attend_kernel(qb, q_ref, k_ref, v_ref, o_ref, l_ref):
    rows = q_ref.shape[0]
    lane = lax.broadcasted_iota(jnp.int32, (qb, 128), 1)
    pair = pl.program_id(0)

    @pl.when(pair == 0)
    def _():
        l_ref[...] = jnp.zeros_like(l_ref)

    def step(i, carry):
        at = pl.ds(pl.multiple_of(i * qb, qb), qb)
        q = q_ref[at, :]
        outs = []
        low = l_ref[at, :]
        for h in range(2):
            own = (lane < HD) if h == 0 else (lane >= HD)
            s = nt(jnp.where(own, q, jnp.zeros_like(q)), k_ref[...])
            m = jnp.max(s, axis=1, keepdims=True)
            e = jnp.exp(s - m)
            t = jnp.sum(e, axis=1, keepdims=True)
            outs.append(nn(e.astype(bf16), v_ref[...]) * (1.0 / t))
            low = jnp.where(lane == 2 * pair + h, m + jnp.log(t), low)
        o_ref[at, :] = jnp.where(lane < HD, outs[0], outs[1]).astype(bf16)
        l_ref[at, :] = low
        return carry

    lax.fori_loop(0, rows // qb, step, 0)


def attend(q, k, v, qb=256):
    rows, total = q.shape[0], k.shape[0]
    qb = min(qb, rows)
    pair_q = pl.BlockSpec((rows, 128), lambda p: (0, p))
    pair_k = pl.BlockSpec((total, 128), lambda p: (0, p))
    return pl.pallas_call(
        functools.partial(attend_kernel, qb),
        grid=(HEADS // 2,),
        in_specs=[pair_q, pair_k, pair_k],
        out_specs=[pair_q, pl.BlockSpec((rows, 128), lambda p: (0, 0))],
        out_shape=[jax.ShapeDtypeStruct((rows, D), bf16), jax.ShapeDtypeStruct((rows, 128), f32)],
        compiler_params=limit(48),
        cost_estimate=cost(16 * rows * total * D, 8 * total * D, HEADS * rows * total),
        name="attend",
    )(q, k, v)


def attend_back_kernel(qb, q_ref, k_ref, v_ref, o_ref, g_ref, l_ref, dq_ref, dk_ref, dv_ref, dk_acc, dv_acc):
    rows = q_ref.shape[0]
    lane = lax.broadcasted_iota(jnp.int32, (qb, 128), 1)
    pair = pl.program_id(0)
    dk_acc[...] = jnp.zeros_like(dk_acc)
    dv_acc[...] = jnp.zeros_like(dv_acc)

    def step(i, carry):
        at = pl.ds(pl.multiple_of(i * qb, qb), qb)
        q = q_ref[at, :]
        g = g_ref[at, :]
        qt = q.astype(f32).T.astype(bf16)
        gt = g.astype(f32).T.astype(bf16)
        prod = o_ref[at, :].astype(f32) * g.astype(f32)
        low = l_ref[at, :]
        dqs = []
        for h in range(2):
            own = (lane < HD) if h == 0 else (lane >= HD)
            lse = jnp.sum(jnp.where(lane == 2 * pair + h, low, 0.0), axis=1, keepdims=True)
            delta = jnp.sum(jnp.where(own, prod, 0.0), axis=1, keepdims=True)
            s = nt(jnp.where(own, q, jnp.zeros_like(q)), k_ref[...])
            p = jnp.exp(s - lse)
            dp = nt(jnp.where(own, g, jnp.zeros_like(g)), v_ref[...])
            ds = (p * (dp - delta)).astype(bf16)
            part = pl.ds(h * HD, HD)
            dv_acc[part, :] += nn(gt[h * HD : (h + 1) * HD, :], p.astype(bf16))
            dk_acc[part, :] += nn(qt[h * HD : (h + 1) * HD, :], ds)
            dqs.append(nn(ds, k_ref[...]))
        dq_ref[at, :] = (jnp.where(lane < HD, dqs[0], dqs[1]) * (HD**-0.5)).astype(bf16)
        return carry

    lax.fori_loop(0, rows // qb, step, 0)
    dk_ref[...] = dk_acc[...].T.astype(bf16)
    dv_ref[...] = dv_acc[...].T.astype(bf16)


def attend_back(q, k, v, o, g, l, qb=512):
    rows, total = q.shape[0], k.shape[0]
    qb = min(qb, rows)
    pair_q = pl.BlockSpec((rows, 128), lambda p: (0, p))
    pair_k = pl.BlockSpec((total, 128), lambda p: (0, p))
    return pl.pallas_call(
        functools.partial(attend_back_kernel, qb),
        grid=(HEADS // 2,),
        in_specs=[pair_q, pair_k, pair_k, pair_q, pair_q, pl.BlockSpec((rows, 128), lambda p: (0, 0))],
        out_specs=[pair_q, pair_k, pair_k],
        out_shape=[
            jax.ShapeDtypeStruct((rows, D), bf16),
            jax.ShapeDtypeStruct((total, D), bf16),
            jax.ShapeDtypeStruct((total, D), bf16),
        ],
        scratch_shapes=[pltpu.VMEM((128, total), f32), pltpu.VMEM((128, total), f32)],
        compiler_params=limit(48),
        cost_estimate=cost(40 * rows * total * D, 16 * total * D, HEADS * rows * total),
        name="attend_back",
    )(q, k, v, o, g, l)


def fold_kernel(w0_ref, w1_ref, w2_ref, hi_ref, lo_ref, vec_ref, coef_ref, low_ref, lowt_ref, key_ref, query_ref):
    head = lax.broadcasted_iota(jnp.int32, (128, D), 0)
    column = lax.broadcasted_iota(jnp.int32, (128, D), 1)
    query = (nn(vec_ref[...].astype(bf16), tile_of(w0_ref))[0:1, :] + vec_ref[1:2, :]).astype(bf16)
    query_ref[...] = jnp.broadcast_to(query.astype(f32), query_ref.shape)
    spread = jnp.where(column // HD == head, query.astype(f32), 0.0).astype(bf16)
    key = nt(spread, tile_of(w1_ref)) * (HD**-0.5)
    key_ref[...] = key[:HEADS]
    key_hi = key.astype(bf16)
    key_lo = (key - key_hi.astype(f32)).astype(bf16)
    coef_ref[...] = nt(hi_ref[...], key_hi) + nt(lo_ref[...], key_hi) + nt(hi_ref[...], key_lo)
    value = tile_of(w2_ref)
    val = nn(hi_ref[...], value) + nn(lo_ref[...], value)
    row = lax.broadcasted_iota(jnp.int32, (TABLE, D), 0)
    val = jnp.where(row >= PIX * VARS, val + vec_ref[2:3, :], val)
    low_ref[...] = val.astype(bf16)
    lowt_ref[...] = val.T.astype(bf16)


def fold(every, hi, lo, vecs):
    return pl.pallas_call(
        fold_kernel,
        grid=(1,),
        in_specs=[*(tile_spec(every, m) for m in range(3)), once((TABLE, D)), once((TABLE, D)), once((8, D))],
        out_specs=[once(s) for s in ((TABLE, 128), (TABLE, D), (D, TABLE), (HEADS, D), (8, D))],
        out_shape=[
            jax.ShapeDtypeStruct((TABLE, 128), f32),
            jax.ShapeDtypeStruct((TABLE, D), bf16),
            jax.ShapeDtypeStruct((D, TABLE), bf16),
            jax.ShapeDtypeStruct((HEADS, D), f32),
            jax.ShapeDtypeStruct((8, D), f32),
        ],
        compiler_params=limit(60),
        cost_estimate=cost(6 * TABLE * D * D, 6 * D * D),
        name="fold",
    )(every, every, every, hi, lo, vecs)


def mix_probs(f, coef_ref, h):
    part = lambda k: coef_ref[k * VARS : (k + 1) * VARS, h : h + 1]
    s = part(PIX)
    for k in range(PIX):
        s = s + part(k) * f[k]
    e = jnp.exp(s - jnp.max(s, axis=0, keepdims=True))
    return e * (1.0 / jnp.sum(e, axis=0, keepdims=True))


def mix_kernel(f_ref, coef_ref, tt_ref, o_ref):
    f = [f_ref[0, k].astype(f32) for k in range(PIX)]

    def one(h):
        pa = mix_probs(f, coef_ref, h)
        pf = jnp.concatenate([pa * x for x in f] + [pa], axis=0).astype(bf16)
        return nn(tt_ref[h * HD : (h + 1) * HD, :], pf)

    for p in range(HEADS // 2):
        both = jnp.concatenate([one(2 * p), one(2 * p + 1)], axis=0)
        o_ref[:, p * 128 : (p + 1) * 128] = both.T.astype(bf16)


def mix(fields, coef, tt):
    nb, _, _, count = fields.shape
    return pl.pallas_call(
        mix_kernel,
        grid=(nb,),
        in_specs=[
            pl.BlockSpec((1, PIX, VARS, count), lambda b: (b, 0, 0, 0)),
            once((TABLE, 128)),
            once((D, TABLE)),
        ],
        out_specs=pl.BlockSpec((count, D), lambda b: (b, 0)),
        out_shape=jax.ShapeDtypeStruct((nb * count, D), bf16),
        compiler_params=limit(40),
        cost_estimate=cost(8 * nb * count * TABLE * D, 4 * nb * count * D, nb * count * VARS * HEADS),
        name="mix",
    )(fields, coef, tt)


def mix_back_kernel(side_ref, f_ref, coef_ref, t_ref, g_ref, rest_ref, mine_ref, other_ref, dt_ref, dc_ref):
    @pl.when(pl.program_id(0) == 0)
    def _():
        dc_ref[...] = jnp.zeros_like(dc_ref)
        dt_ref[...] = jnp.zeros_like(dt_ref)

    lane = lax.broadcasted_iota(jnp.int32, (VARS, 128), 1)
    f = [f_ref[0, k].astype(f32) for k in range(PIX)]
    for h in range(HEADS):
        pair = slice(h // 2 * 128, h // 2 * 128 + 128)
        own = (lane[:1] < HD) if h % 2 == 0 else (lane[:1] >= HD)
        pa = mix_probs(f, coef_ref, h)
        pf = jnp.concatenate([pa * x for x in f] + [pa], axis=0).astype(bf16)
        g = jnp.where(own, g_ref[:, pair], jnp.zeros((), bf16))
        dpf = nt(t_ref[:, pair], g)
        dpa = dpf[PIX * VARS :]
        for k in range(PIX):
            dpa = dpa + dpf[k * VARS : (k + 1) * VARS] * f[k]
        ds = pa * (dpa - jnp.sum(pa * dpa, axis=0, keepdims=True))
        for k in range(PIX + 1):
            w = ds * f[k] if k < PIX else ds
            dc_ref[k * VARS : (k + 1) * VARS, :] += jnp.where(lane == h, jnp.sum(w, axis=1, keepdims=True), 0.0)
        dt_ref[:, pair] += nn(pf, g)

    @pl.when(pl.program_id(0) == pl.num_programs(0) - 1)
    def _():
        dct = jnp.concatenate([dc_ref[...].T[:HEADS], jnp.zeros((HEADS, D // 2 - TABLE), f32)], axis=1)
        half = D // 2
        for at, left, right in (
            (0, dt_ref[:, :half], dt_ref[:, half:]),
            (TABLE, dct, jnp.zeros_like(dct)),
            (TABLE + HEADS, rest_ref[:, :half], rest_ref[:, half:]),
        ):
            rows = slice(at, at + left.shape[0])
            first = side_ref[0] == 0
            mine_ref[rows, :] = jnp.where(first, left, right)
            other_ref[rows, :] = jnp.where(first, right, left).astype(bf16)


def mix_back(side, fields, coef, t, g, rest):
    nb, _, _, count = fields.shape
    shape = (TABLE + HEADS + rest.shape[0], D // 2)
    whole = lambda s: pl.BlockSpec(s, lambda b: (0,) * len(s))
    return pl.pallas_call(
        mix_back_kernel,
        grid=(nb,),
        in_specs=[
            pl.BlockSpec(memory_space=pltpu.SMEM),
            pl.BlockSpec((1, PIX, VARS, count), lambda b: (b, 0, 0, 0)),
            once((TABLE, 128)),
            once((TABLE, D)),
            pl.BlockSpec((count, D), lambda b: (b, 0)),
            once(rest.shape),
        ],
        out_specs=[whole(shape), whole(shape)],
        out_shape=[jax.ShapeDtypeStruct(shape, f32), jax.ShapeDtypeStruct(shape, bf16)],
        scratch_shapes=[pltpu.VMEM((TABLE, D), f32), pltpu.VMEM((TABLE, 128), f32)],
        compiler_params=limit(40),
        cost_estimate=cost(16 * nb * count * TABLE * D, 4 * nb * count * D, nb * count * VARS * HEADS),
        name="mix_back",
    )(side, fields, coef, t, g, rest)


def front_kernel(m_ref, w3_ref, w4_ref, w5_ref, w6_ref, row_ref, col_ref, vec_ref, h_ref, a_ref, q_ref, k_ref, v_ref):
    per = row_ref.shape[1]
    h = nn(m_ref[...], tile_of(w3_ref))
    h = h + jnp.concatenate([col_ref[...] + row_ref[0, i : i + 1, :] for i in range(per)], axis=0)
    h_ref[...] = h
    center = h - jnp.mean(h, axis=-1, keepdims=True)
    inverse = lax.rsqrt(jnp.mean(center * center, axis=-1, keepdims=True) + norm_eps)
    a = (center * inverse * vec_ref[0:1, :] + vec_ref[1:2, :]).astype(bf16)
    a_ref[...] = a
    k_ref[...] = nn(a, tile_of(w5_ref)).astype(bf16)
    v_ref[...] = (nn(a, tile_of(w6_ref)) + vec_ref[3:4, :]).astype(bf16)

    @pl.when(pl.program_id(0) == 0)
    def _():
        q_ref[...] = ((nn(a, tile_of(w4_ref)) + vec_ref[2:3, :]) * (HD**-0.5)).astype(bf16)


def front(mixed, every, row, col, vecs, blocks):
    total = mixed.shape[0]
    count = total // blocks
    per = row.shape[0] // blocks
    block = pl.BlockSpec((count, D), lambda b: (b, 0))
    return pl.pallas_call(
        front_kernel,
        grid=(blocks,),
        in_specs=[
            block,
            *(tile_spec(every, m) for m in range(3, 7)),
            pl.BlockSpec((1, per, D), lambda b: (b, 0, 0)),
            once(col.shape),
            once(vecs.shape),
        ],
        out_specs=[block, block, pl.BlockSpec((count, D), lambda b: (0, 0)), block, block],
        out_shape=[
            jax.ShapeDtypeStruct((total, D), f32),
            jax.ShapeDtypeStruct((total, D), bf16),
            jax.ShapeDtypeStruct((count, D), bf16),
            jax.ShapeDtypeStruct((total, D), bf16),
            jax.ShapeDtypeStruct((total, D), bf16),
        ],
        compiler_params=limit(52),
        cost_estimate=cost(6 * total * D * D, 16 * total * D),
        name="front",
    )(mixed, *[every] * 4, row.reshape(blocks, per, D), col, vecs)


def norm_parts(values):
    center = values - jnp.mean(values, axis=-1, keepdims=True)
    inverse = lax.rsqrt(jnp.mean(center * center, axis=-1, keepdims=True) + norm_eps)
    return center * inverse, inverse


def norm_grad(grad, normed, inverse, gain):
    scaled = grad * gain
    return inverse * (
        scaled
        - jnp.mean(scaled, axis=-1, keepdims=True)
        - normed * jnp.mean(scaled * normed, axis=-1, keepdims=True)
    )


def column_sum(array):
    return jnp.sum(array, axis=0, keepdims=True)


def mlp_kernel(h0_ref, att_ref, wo_ref, one_ref, two_ref, vec_ref, head_ref, target_ref, factor_ref,
               act_ref, a2_ref, dh2_ref, du_ref, dh1_ref, dh1_low_ref, datt_ref, dhead_ref, sum_ref, loss_ref,
               h1, acc, grad2, slope):
    i = pl.program_id(0)
    folds = slope.shape[0]
    f = jnp.where(i < folds, i, 2 * folds - 1 - i)
    gain2, shift2, bias2, gain3, shift3 = [vec_ref[r : r + 1, :] for r in range(5)]

    @pl.when(i == 0)
    def _():
        h1[...] = h0_ref[...] + nn(att_ref[...], tile_of(wo_ref))
        normed, _ = norm_parts(h1[...])
        a2_ref[...] = (normed * gain2 + shift2).astype(bf16)
        acc[...] = h1[...] + bias2
        sum_ref[...] = jnp.zeros_like(sum_ref)

    @pl.when(i < folds)
    def _():
        u = nn(a2_ref[...], tile_of(one_ref)) + vec_ref[pl.ds(8 + f, 1), :]
        phi = 0.5 * (1.0 + lax.erf(u * 0.7071067811865476))
        slope[f] = phi + u * jnp.exp(-0.5 * u * u) * 0.3989422804014327
        act = (u * phi).astype(bf16)
        act_ref[...] = act
        acc[...] += nn(act, tile_of(two_ref))

    @pl.when(i == folds - 1)
    def _():
        normed, inverse = norm_parts(acc[...])
        z = (normed * gain3 + shift3).astype(bf16)
        error = nt(z, head_ref[...]) - target_ref[...]
        weighted = factor_ref[...] * error
        loss_ref[...] = jnp.broadcast_to(jnp.sum(column_sum(weighted * error), axis=1, keepdims=True), loss_ref.shape)
        dpred = (2.0 * weighted).astype(bf16)
        dhead_ref[...] = lax.dot_general(dpred, z, (((0,), (0,)), ((), ())), preferred_element_type=f32)
        dz = nn(dpred, head_ref[...])
        sum_ref[1:2, :] = column_sum(dz * normed)
        sum_ref[2:3, :] = column_sum(dz)
        grad = norm_grad(dz, normed, inverse, gain3)
        sum_ref[0:1, :] = column_sum(grad)
        grad2[...] = grad
        dh2_ref[...] = grad.astype(bf16)
        acc[...] = jnp.zeros_like(acc)

    @pl.when(i >= folds)
    def _():
        du = nt(dh2_ref[...], tile_of(two_ref)) * slope[f]
        sum_ref[pl.ds(6 + f, 1), :] = column_sum(du)
        low = du.astype(bf16)
        du_ref[...] = low
        acc[...] += nt(low, tile_of(one_ref))

    @pl.when(i == 2 * folds - 1)
    def _():
        normed, inverse = norm_parts(h1[...])
        grad = acc[...]
        sum_ref[3:4, :] = column_sum(grad * normed)
        sum_ref[4:5, :] = column_sum(grad)
        grad = grad2[...] + norm_grad(grad, normed, inverse, gain2)
        dh1_ref[...] = grad
        low = grad.astype(bf16)
        dh1_low_ref[...] = low
        datt_ref[...] = nt(low, tile_of(wo_ref)).astype(bf16)


def mlp(hidden0, attended, first, second, vecs, head, targets, factor):
    count, width = targets.shape
    folds = FF // D
    fold = lambda i: jnp.where(i < folds, i, 2 * folds - 1 - i)
    tile = lambda base: pl.BlockSpec(
        second.shape[:2] + (1,) + second.shape[3:], lambda i: (0, 0, base + fold(i), 0, 0)
    )
    fixed = lambda s: pl.BlockSpec(s, lambda i: (0,) * len(s))
    state = (count, D)
    return pl.pallas_call(
        mlp_kernel,
        grid=(2 * folds,),
        in_specs=[
            once(state), once(state), tile_spec(first, 7), tile(0), tile(folds), once(vecs.shape), once(head.shape),
            once(targets.shape), once(factor.shape),
        ],
        out_specs=[
            pl.BlockSpec(state, lambda i: (0, jnp.minimum(i, folds - 1))),
            fixed(state),
            fixed(state),
            pl.BlockSpec(state, lambda i: (0, jnp.minimum(2 * folds - 1 - i, folds - 1))),
            fixed(state),
            fixed(state),
            fixed(state),
            fixed(head.shape),
            fixed((16, D)),
            fixed((8, 128)),
        ],
        out_shape=[
            jax.ShapeDtypeStruct((count, FF), bf16),
            jax.ShapeDtypeStruct(state, bf16),
            jax.ShapeDtypeStruct(state, bf16),
            jax.ShapeDtypeStruct((count, FF), bf16),
            jax.ShapeDtypeStruct(state, f32),
            jax.ShapeDtypeStruct(state, bf16),
            jax.ShapeDtypeStruct(state, bf16),
            jax.ShapeDtypeStruct(head.shape, f32),
            jax.ShapeDtypeStruct((16, D), f32),
            jax.ShapeDtypeStruct((8, 128), f32),
        ],
        scratch_shapes=[
            pltpu.VMEM(state, f32), pltpu.VMEM(state, f32), pltpu.VMEM(state, f32), pltpu.VMEM((folds,) + state, f32)
        ],
        compiler_params=limit(60),
        cost_estimate=cost(8 * count * D * FF, 20 * D * FF, 2 * count * FF),
        name="mlp",
    )(hidden0, attended, first, second, second, vecs, head, targets, factor)


def back_kernel(dq_ref, dk_ref, dv_ref, h_ref, dh_ref, w3_ref, w4_ref, w5_ref, w6_ref, vec_ref, g_ref, gm_ref, sum_ref, acc):
    first = pl.program_id(0) == 0
    acc[...] = nt(dk_ref[...], tile_of(w5_ref)) + nt(dv_ref[...], tile_of(w6_ref))

    @pl.when(first)
    def _():
        sum_ref[...] = jnp.zeros_like(sum_ref)
        acc[...] += nt(dq_ref[...], tile_of(w4_ref))
        sum_ref[4:5, :] = jnp.sum(dq_ref[...].astype(f32), axis=0, keepdims=True)

    h = h_ref[...]
    center = h - jnp.mean(h, axis=-1, keepdims=True)
    inverse = lax.rsqrt(jnp.mean(center * center, axis=-1, keepdims=True) + norm_eps)
    normed = center * inverse
    grad = acc[...]
    sum_ref[1:2, :] += jnp.sum(grad * normed, axis=0, keepdims=True)
    sum_ref[2:3, :] += jnp.sum(grad, axis=0, keepdims=True)
    sum_ref[3:4, :] += jnp.sum(dv_ref[...].astype(f32), axis=0, keepdims=True)
    scaled = grad * vec_ref[0:1, :]
    out = inverse * (
        scaled
        - jnp.mean(scaled, axis=-1, keepdims=True)
        - normed * jnp.mean(scaled * normed, axis=-1, keepdims=True)
    )
    acc[...] = out

    @pl.when(first)
    def _():
        acc[...] += dh_ref[...]

    out = acc[...]
    sum_ref[0:1, :] += jnp.sum(out, axis=0, keepdims=True)
    low = out.astype(bf16)
    g_ref[...] = low
    gm_ref[...] = nt(low, tile_of(w3_ref)).astype(bf16)


def back(dq, dk, dv, h, dh, every, vecs, blocks):
    total = dk.shape[0]
    count = total // blocks
    block = pl.BlockSpec((count, D), lambda b: (b, 0))
    return pl.pallas_call(
        back_kernel,
        grid=(blocks,),
        in_specs=[
            once((count, D)),
            block,
            block,
            block,
            once((count, D)),
            *(tile_spec(every, m) for m in range(3, 7)),
            once(vecs.shape),
        ],
        out_specs=[block, block, pl.BlockSpec((8, D), lambda b: (0, 0))],
        out_shape=[
            jax.ShapeDtypeStruct((total, D), bf16),
            jax.ShapeDtypeStruct((total, D), bf16),
            jax.ShapeDtypeStruct((8, D), f32),
        ],
        scratch_shapes=[pltpu.VMEM((count, D), f32)],
        compiler_params=limit(52),
        cost_estimate=cost(7 * total * D * D, 16 * total * D),
        name="back",
    )(dq, dk, dv, h, dh, *[every] * 4, vecs)


def choose_kernel(first, slot_ref, p_ref, wait_ref, out_ref):
    for m in range(out_ref.shape[0]):
        out_ref[m] = p_ref[slot_ref[first + m]]


def choose(slot_of, pieces, first, count, wait):
    shape = (count,) + pieces.shape[1:]
    whole = lambda s: pl.BlockSpec(s, lambda i, at: (0, 0, 0))
    return pl.pallas_call(
        functools.partial(choose_kernel, first),
        grid_spec=pltpu.PrefetchScalarGridSpec(
            num_scalar_prefetch=1,
            grid=(1,),
            in_specs=[whole(pieces.shape), pl.BlockSpec(memory_space=pltpu.HBM)],
            out_specs=whole(shape),
        ),
        out_shape=jax.ShapeDtypeStruct(shape, pieces.dtype),
        compiler_params=limit(60),
        cost_estimate=cost(0, 4 * pieces.size),
        name="choose",
    )(slot_of, pieces, wait)


def finish_kernel(plan, slot_ref, *refs):
    ins, out, square = refs[:-2], refs[-2], refs[-1]
    half = out.shape[2]
    for m in range(3):
        out[slot_ref[m]] = jnp.zeros_like(out[0])
    total = jnp.zeros(out.shape[1:], f32)
    ins = list(ins)
    for per, tiles in plan:
        job, ins = ins[:per], ins[per:]
        for m, index, col in tiles:
            parts = [r[index, :, col * half : (col + 1) * half].astype(f32) for r in job]
            value = sum(parts[1:], parts[0])
            out[slot_ref[m]] = value.astype(out.dtype)
            total = total + value * value
    square[...] = jnp.sum(total.reshape(total.shape[0] // 8, 8, half), axis=0)


def finish(slot_of, plan, jobs):
    arrays = [a for job in jobs for a in job]
    plan = tuple((len(job), tiles) for job, tiles in zip(jobs, plan))
    rows, half = arrays[0].shape[1], D // 2
    whole = lambda s: pl.BlockSpec(s, lambda i, at: (0,) * len(s))
    n = slot_of.shape[0]
    return pl.pallas_call(
        functools.partial(finish_kernel, plan),
        grid_spec=pltpu.PrefetchScalarGridSpec(
            num_scalar_prefetch=1,
            grid=(1,),
            in_specs=[whole(a.shape) for a in arrays],
            out_specs=[whole((n, rows, half)), whole((8, half))],
        ),
        out_shape=[jax.ShapeDtypeStruct((n, rows, half), bf16), jax.ShapeDtypeStruct((8, half), f32)],
        compiler_params=limit(48),
        cost_estimate=cost(0, 3 * 4 * n * rows * half),
        name="finish",
    )(slot_of, *arrays)


beta_one = 0.9
beta_two = 0.95
rate_tiles = 0.01
rate_vectors = 0.1
decay_weight = 1e-05
adam_eps = 1e-08
STEP = 10
clip_norm = 0.02


def adam_update(weight, grad, first, second, rate):
    first = beta_one * first + (1.0 - beta_one) * grad
    second = beta_two * second + (1.0 - beta_two) * grad * grad
    first_hat = first / (1.0 - beta_one**STEP)
    second_hat = second / (1.0 - beta_two**STEP)
    weight = weight - rate * (first_hat / (jnp.sqrt(second_hat) + adam_eps) + decay_weight * weight)
    return (weight, first, second)


def tail_kernel(square_ref, w0_ref, w1_ref, w2_ref, hi_ref, lo_ref, gram_ref, key_ref, query_ref, vec_ref, late_ref,
                p_ref, m_ref, v_ref, clip_ref, gkey_ref, agg_ref, p_new, m_new, v_new, ge, extra):
    head = lax.broadcasted_iota(jnp.int32, (HEADS, D), 0)
    column = lax.broadcasted_iota(jnp.int32, (HEADS, D), 1)

    def parts(a):
        high = a.astype(bf16)
        return high, (a - high.astype(f32)).astype(bf16)

    def tn(a, b):
        return lax.dot_general(a, b, (((0,), (0,)), ((), ())), preferred_element_type=f32)

    offset = PIX * VARS
    fold_ref, head_ref = late_ref.at[0:TABLE, :], late_ref.at[TABLE + 40 : TABLE + 40 + offset, :]
    coef_hi, coef_lo = parts(late_ref[TABLE : TABLE + HEADS, 0:256][:, :TABLE])
    grad_key = (nn(coef_hi, hi_ref[...]) + nn(coef_hi, lo_ref[...]) + nn(coef_lo, hi_ref[...])) * (HD**-0.5)
    gkey_ref[...] = grad_key
    key_hi, key_lo = parts(grad_key)
    by_head = nn(key_hi, tile_of(w1_ref)) + nn(key_lo, tile_of(w1_ref))
    agg = jnp.sum(jnp.where(column // HD == head, by_head, 0.0), axis=0, keepdims=True)
    agg_ref[...] = jnp.broadcast_to(agg, agg_ref.shape)
    agg_hi, agg_lo = parts(jnp.broadcast_to(agg, (8, D)))
    by_query = (nt(agg_hi, tile_of(w0_ref)) + nt(agg_lo, tile_of(w0_ref)))[0:1]
    fold_hi, fold_lo = parts(fold_ref[...])
    fold_key_hi, fold_key_lo = parts(key_ref[...])
    ge[...] = (
        nt(fold_hi, tile_of(w2_ref)) + nt(fold_lo, tile_of(w2_ref))
        + tn(coef_hi, fold_key_hi) + tn(coef_hi, fold_key_lo) + tn(coef_lo, fold_key_hi)
    )
    rest = late_ref[TABLE + HEADS : TABLE + HEADS + 24, :]
    order = [
        by_query, rest[5:6], rest[0:1], agg, jnp.sum(fold_ref[offset:, :], axis=0, keepdims=True), rest[0:1],
        rest[1:2], rest[2:3], rest[4:5], rest[3:4], rest[11:12], rest[12:13], rest[8:9], rest[9:10], rest[10:11],
    ]
    for i, r in enumerate(order):
        extra[i : i + 1, :] = r
    extra[15:19, :] = rest[14:18]
    gram_hi, gram_lo = parts(gram_ref[...])
    through = nn(gram_hi, fold_hi) + nn(gram_hi, fold_lo) + nn(gram_lo, fold_hi)
    total = jnp.sum(through * fold_ref[...], axis=0, keepdims=True)
    total += jnp.sum(ge[...] * ge[...], axis=0, keepdims=True)
    bias = ge[offset:, :]
    total += jnp.sum(bias * bias, axis=0, keepdims=True)
    total += jnp.sum(head_ref[...] * head_ref[...], axis=0, keepdims=True)
    total += jnp.sum(extra[0:19, :] * extra[0:19, :], axis=0, keepdims=True)
    vq = vec_ref[0:1, :].astype(bf16).astype(f32)
    total = jnp.sum(total, axis=1, keepdims=True)
    total += jnp.sum(vq * vq, axis=1, keepdims=True) * jnp.sum(agg * agg, axis=1, keepdims=True)
    query = query_ref[0:1, :]
    per_head = jnp.sum(jnp.where(column // HD == head, query * query, 0.0), axis=1, keepdims=True)
    total += jnp.sum(jnp.sum(grad_key * grad_key, axis=1, keepdims=True) * per_head, axis=0, keepdims=True)
    norm = jnp.sqrt(total + square_ref[0])
    clip = jnp.minimum(1.0, clip_norm / (norm + 1e-06))
    lane = lax.broadcasted_iota(jnp.int32, (8, 128), 1)
    clip_ref[...] = jnp.where(lane == 0, clip, norm)

    def update(rows, grad):
        p_new[rows, :], m_new[rows, :], v_new[rows, :] = adam_update(
            p_ref[rows, :], grad * clip, m_ref[rows, :], v_ref[rows, :], rate_vectors
        )

    for k in range(PIX):
        for v in range(VARS):
            extra_row = 32 + v * PIX + k
            extra[extra_row : extra_row + 1, :] = ge[k * VARS + v : k * VARS + v + 1, :]
    update(pl.ds(0, offset), extra[32 : 32 + offset, :])
    update(pl.ds(offset, VARS), bias)
    update(pl.ds(offset + VARS, VARS), bias)
    update(pl.ds(offset + 2 * VARS, offset), head_ref[...])
    update(pl.ds(2 * offset + 2 * VARS, 19), extra[0:19, :])


def tail(square, every, hi, lo, gram, key, query, vecs, late, w, m, v):
    vmem = pl.BlockSpec(memory_space=pltpu.VMEM)
    arrays = (hi, lo, gram, key, query, vecs, late, w, m, v)
    return pl.pallas_call(
        tail_kernel,
        grid=(1,),
        in_specs=[pl.BlockSpec(memory_space=pltpu.SMEM), *(tile_spec(every, m) for m in range(3))]
        + [once(a.shape) for a in arrays],
        out_specs=[once(s) for s in ((8, 128), (HEADS, D), (8, D), w.shape, w.shape, w.shape)],
        out_shape=[
            jax.ShapeDtypeStruct(s, f32) for s in ((8, 128), (HEADS, D), (8, D), w.shape, w.shape, w.shape)
        ],
        scratch_shapes=[pltpu.VMEM((TABLE, D), f32), pltpu.VMEM((32 + PIX * VARS, D), f32)],
        compiler_params=limit(36),
        cost_estimate=cost(8 * TABLE * D * D, 28 * w.size),
        name="tail",
    )(square, every, every, every, *arrays)


PROWS = 32
PCOLS = 64
GROUPS = 5
HIGHEST = lax.Precision.HIGHEST
clip_norm = 0.02
SCALE = HD**-0.5


def position_parts():
    quarter = D // 4
    omega = jnp.exp(-math.log(10000.0) * jnp.arange(quarter).astype(f32) / quarter)
    row = jnp.arange(PROWS).astype(f32)[:, None] * omega[None, :]
    col = jnp.arange(PCOLS).astype(f32)[:, None] * omega[None, :]
    zero_row = jnp.zeros((PROWS, D // 2), f32)
    zero_col = jnp.zeros((PCOLS, D // 2), f32)
    row_part = jnp.concatenate([jnp.sin(row), jnp.cos(row), zero_row], axis=1)
    col_part = jnp.concatenate([zero_col, jnp.sin(col), jnp.cos(col)], axis=1)
    return row_part, col_part


def latitude_table(start, count):
    index = start + jnp.arange(count)
    inner = jnp.arange(PIX) // 2
    lat_rows = 2 * (index // PCOLS)[:, None] + inner[None, :]
    total_rows = 2 * PROWS
    angle = (lat_rows.astype(f32) + 0.5) * (math.pi / total_rows) - math.pi / 2
    every = (jnp.arange(total_rows).astype(f32) + 0.5) * (math.pi / total_rows) - math.pi / 2
    weight = jnp.cos(angle) / jnp.mean(jnp.cos(every))
    return jnp.tile(weight, (1, VARS))


def tn(left, right):
    return lax.dot_general(left, right, (((0,), (0,)), ((), ())), preferred_element_type=f32)


def split_low(values):
    high = lax.reduce_precision(values, 8, 7)
    return high.astype(bf16), (values - high).astype(bf16)


def swap(array, bit):
    n = lax.axis_size("dp")
    return lax.ppermute(array, "dp", [(i, i ^ bit) for i in range(n)])


def shift(array, step):
    n = lax.axis_size("blk")
    return lax.ppermute(array, "blk", [(i, (i + step) % n) for i in range(n)])


def dp_bits():
    return [1 << i for i in range(lax.axis_size("dp").bit_length() - 1)]


def after(array, *others):
    return lax.optimization_barrier((array, *others))[0]


def pick(array, axis, index):
    return lax.dynamic_index_in_dim(array, index, axis, False)


def halves(array, side):
    half = array.shape[-1] // 2
    left, right = array[..., :half], array[..., half:]
    return jnp.where(side == 0, left, right), jnp.where(side == 0, right, left)


def sum_small(values):
    n_dp, blocks = lax.axis_size("dp"), lax.axis_size("blk")
    me = lax.axis_index("blk") * n_dp + lax.axis_index("dp")
    width = -(-n_dp * blocks // 128) * 128
    array = jnp.where(jnp.arange(width)[None, :] == me, values[:, None], 0.0)
    array = sum([shift(array, k) for k in range(1, blocks)], array)
    array = sum([swap(array, 2 * mask) for mask in range(1, n_dp // 2)], array)
    return jnp.sum(array + swap(array, 1), axis=1)


def gather_blocks(array):
    n = lax.axis_size("blk")
    return jnp.stack([array] + [shift(array, k) for k in range(1, n)])


def gather(pieces):
    blocks, n_dp = lax.axis_size("blk"), lax.axis_size("dp")
    return lax.all_gather(pieces, ("blk", "dp"), axis=0).reshape((blocks, n_dp) + pieces.shape)


class SplitSum:
    def __init__(self, cur, order, low=True):
        self.blocks = lax.axis_size("blk")
        self.left = list(reversed(dp_bits()[1:]))
        rows = cur.shape[1] // (self.blocks << len(self.left))
        self.cur = cur.reshape((cur.shape[0], self.blocks) + (2,) * len(self.left) + (rows,) + cur.shape[2:])
        self.order = list(order)
        self.type = bf16 if low else f32
        self.got = []

    @classmethod
    def joined(cls, jobs):
        job = cls.__new__(cls)
        for other in jobs:
            other.take()
        job.blocks, job.type, job.got = jobs[0].blocks, jobs[0].type, []
        job.cur = jnp.concatenate([other.cur for other in jobs], axis=0)
        return job

    def take(self):
        for got in self.got:
            self.cur = self.cur + got.astype(f32)
        self.got = []

    def send(self):
        self.take()
        bit = self.order.pop(0)
        axis = 2 + self.left.index(bit)
        mine = (lax.axis_index("dp") // bit) % 2
        sent = pick(self.cur, axis, 1 - mine).astype(self.type)
        self.cur = pick(self.cur, axis, mine)
        self.left.remove(bit)
        self.got = [swap(sent, bit)]
        return sent

    def send_all(self):
        self.take()
        order, n, at = self.order, 1 << len(self.left), 2
        own = lax.axis_index("dp") // 2
        cur = self.cur.reshape(self.cur.shape[:2] + (n,) + self.cur.shape[2 + len(self.left) :])
        sent = [pick(cur, at, own ^ mask).astype(self.type) for mask in range(1, n)]
        self.cur, self.order, self.left = pick(cur, at, own), [], []
        self.got = [swap(a, 2 * (i + 1)) for i, a in enumerate(sent)]
        return sent

    def send_blocks(self):
        self.take()
        blk = lax.axis_index("blk")
        sent = [pick(self.cur, 1, (blk + k) % self.blocks).astype(self.type) for k in range(1, self.blocks)]
        self.cur = pick(self.cur, 1, blk)
        self.got = [shift(a, k + 1) for k, a in enumerate(sent)]
        return sent

    def parts(self):
        return [self.cur, *self.got]

    def end(self):
        for got in self.got:
            self.cur = self.cur + got.astype(f32)
        self.got = []
        return self.cur


class SumRows:
    def __init__(self, mine, other):
        self.rows = mine.shape[0]
        self.side = lax.axis_index("dp") % 2
        self.job = SplitSum((mine + swap(other, 1).astype(f32))[None], dp_bits()[1:])
        self.steps = [self.job.send_all, self.job.send_blocks, self.widen_blocks, self.widen, self.close]

    def step(self):
        return self.steps.pop(0)()

    def widen_blocks(self):
        part = self.job.end()[0].astype(bf16)
        n, blk = lax.axis_size("blk"), lax.axis_index("blk")
        cur = gather_blocks(part)
        self.cur = jnp.stack([pick(cur, 0, (blk - z + n) % n) for z in range(n)])

    def widen(self):
        n, own = lax.axis_size("dp") // 2, lax.axis_index("dp") // 2
        every = jnp.stack([self.cur] + [swap(self.cur, 2 * mask) for mask in range(1, n)])
        self.cur = jnp.stack([pick(every, 0, own ^ i) for i in range(n)], axis=1).reshape(self.rows, -1)

    def close(self):
        cur, got = self.cur, swap(self.cur, 1)
        whole = jnp.where(self.side == 0, jnp.concatenate([cur, got], 1), jnp.concatenate([got, cur], 1))
        return whole.astype(f32)

    def end(self):
        while len(self.steps) > 1:
            self.step()
        return self.step()


def shards(fields, targets, lead_time, pixel_mask, group_id, slot_of, tiles, tiles_m, tiles_v, vectors, vec_m, vec_v):
    _, count, _ = fields.shape
    blocks, n_dp = lax.axis_size("blk"), lax.axis_size("dp")
    total = count * blocks
    folds = FF // D
    dp, blk = lax.axis_index("dp"), lax.axis_index("blk")
    side = dp % 2
    start = blk * count
    others = dp_bits()[1:]
    first_order, second_order = tuple(others), tuple(reversed(others))
    slots, tall, _ = tiles.shape
    n_tiles = slots * n_dp
    rows = 2 * tall // n_dp
    half = D // 2
    fine = tall // n_dp % 16 == 0

    mask_float = pixel_mask[0].astype(f32)
    var_local = jnp.sum(jnp.sum(mask_float, axis=0).reshape(VARS, PIX), axis=1)
    group_hot = (group_id[0] == jnp.arange(GROUPS)).astype(f32)
    counted = sum_small(jnp.pad(jnp.concatenate([var_local, group_hot]), (0, 64 - VARS - GROUPS)))
    field_t = fields[0].astype(bf16).reshape(count, VARS, PIX).transpose(2, 1, 0)
    field_all = gather_blocks(field_t)

    if fine:
        low_rows = tall // n_dp
        pieces = tiles.astype(bf16).reshape(slots, n_dp, low_rows, D)
        pieces = lax.all_to_all(pieces, "dp", 1, 0, tiled=True).reshape(n_tiles, low_rows, D)
        first = gather(choose(slot_of, pieces, 0, 8, slot_of))
        first, field_all = lax.optimization_barrier((first, field_all))
    else:
        slots_low = lax.all_gather(tiles.astype(bf16), "blk", axis=1, tiled=True)
        slots_low = lax.all_gather(slots_low, "dp", axis=0, tiled=True)
        weights = [pick(slots_low, 0, slot_of[m]) for m in range(n_tiles)]
        first = jnp.stack(weights[:8])[None, None]
        second = jnp.stack(weights[8:])[None, None]

    var_total, group_total = counted[:VARS], counted[VARS : VARS + GROUPS] / blocks
    sample_weight = jnp.sum(group_total) / (GROUPS * jnp.sum(group_hot * group_total))
    count_pixels = VARS * jnp.repeat(var_total, PIX)
    factor = sample_weight * mask_float * latitude_table(start, count) / count_pixels

    offset = VARS * PIX
    embed_weight = vectors[:offset].reshape(VARS, PIX, D).transpose(1, 0, 2).reshape(offset, D)
    embed_bias = vectors[offset : offset + VARS] + vectors[offset + VARS : offset + 2 * VARS]
    embed = jnp.concatenate([embed_weight, embed_bias], axis=0)
    head_low = vectors[offset + 2 * VARS : 2 * offset + 2 * VARS].astype(bf16)
    extras = vectors[2 * offset + 2 * VARS :]
    gram = lax.dot_general(embed, embed, NT, precision=HIGHEST, preferred_element_type=f32)
    embed_hi, embed_lo = split_low(embed)

    fold_vecs = jnp.concatenate([extras[0:1], extras[3:5], jnp.zeros((5, D), f32)], axis=0)
    fold_vecs = after(fold_vecs, counted, field_all[:, 0, :8, :128])
    coef, fold_low, fold_low_t, fold_key, query_f = fold(first, embed_hi, embed_lo, fold_vecs)
    if fine:
        second = gather(choose(slot_of, pieces, 8, 8, first))
    mixed = mix(field_all, coef, fold_low_t)

    row_part, col_part = position_parts()
    row_part = row_part.reshape(blocks, PROWS // blocks, D)
    row_here = jnp.concatenate([pick(row_part, 0, (blk - k + blocks) % blocks) for k in range(blocks)], axis=0)
    lead_row = extras[5] + lead_time[0] * extras[1] + extras[2]
    vecs = jnp.concatenate([extras[6:10], jnp.zeros((4, D), f32)], axis=0)
    hidden0, normed1_low, query_blk, key_all, value_all = front(
        mixed, first, row_here + lead_row, col_part, vecs, blocks
    )
    own1_low = normed1_low[:count]
    attended_low, log_total = attend(query_blk, key_all, value_all)

    mlp_vecs = jnp.concatenate([extras[10:15], jnp.zeros((3, D), f32), extras[15 : 15 + folds], jnp.zeros((4, D), f32)], axis=0)
    (activ_low, normed2_low, grad_h2_low, grad_pre_low, grad_h1, grad_h1_low, grad_attended, grad_head, mlp_sums,
     loss_local) = mlp(hidden0, attended_low, first, second, mlp_vecs, head_low, targets[0], factor)
    loss_local = loss_local[0, 0]

    def weight_grads(left, mine, other):
        sent = tn(left, other).astype(bf16)
        return tn(left, mine), swap(sent, 1), sent

    both = lambda parts: parts[0] + parts[1].astype(f32)
    if fine:
        two_parts = weight_grads(activ_low, *halves(grad_h2_low, side))
        left, right = [
            jnp.concatenate([grad_pre_low[:, f * D + s * half : f * D + (s + 1) * half] for f in range(folds)], axis=1)
            for s in range(2)
        ]
        one_parts = weight_grads(normed2_low, jnp.where(side == 0, left, right), jnp.where(side == 0, right, left))
        two_job = SplitSum(both(two_parts).reshape(folds, D, half), first_order)
        one_job = SplitSum(both(one_parts)[None], second_order)
    early = jnp.concatenate([mlp_sums, grad_head], axis=0)
    if fine:
        grad_attended = after(grad_attended, two_job.send(), one_job.send(), early)
    grad_query, grad_keys, grad_values = attend_back(query_blk, key_all, value_all, attended_low, grad_attended, log_total)
    if fine:
        sent = [two_job.send(), one_job.send()]
        grad_query, grad_keys, grad_values, *_ = lax.optimization_barrier((grad_query, grad_keys, grad_values, *sent))
        query_parts = weight_grads(own1_low, *halves(grad_query, side))
        out_parts = weight_grads(attended_low, *halves(grad_h1_low, side))
        key_parts = weight_grads(normed1_low, *halves(grad_keys, side))
        value_parts = weight_grads(normed1_low, *halves(grad_values, side))
        pair_job = SplitSum(jnp.stack([both(key_parts), both(value_parts)]), second_order)
        end_job = SplitSum(jnp.stack([both(query_parts), both(out_parts)]), first_order)
        grad_query = after(grad_query, pair_job.send(), end_job.send())
    grad_h0_low, grad_mixed, sums = back(grad_query, grad_keys, grad_values, hidden0, grad_h1, first, vecs, blocks)
    sums = jnp.where(jnp.arange(8)[:, None] == 5, sums[0] * lead_time[0], sums)
    step = 16 * (n_dp // 2) * blocks
    below = sums.shape[0] + early.shape[0]
    rest = jnp.concatenate([sums, early, jnp.zeros((-(TABLE + HEADS + below) % step, D), f32)], axis=0)
    if fine:
        sent = [pair_job.send(), end_job.send(), *two_job.send_blocks(), *one_job.send_blocks(), rest]
        grad_h0_low, grad_mixed, *_, rest = lax.optimization_barrier((grad_h0_low, grad_mixed, *sent))
        agg_parts = weight_grads(mixed, *halves(grad_h0_low, side))
        agg_job = SplitSum(both(agg_parts)[None], first_order)
        grad_mixed = after(grad_mixed, agg_parts[2])
    late_mine, late_other = mix_back(side.reshape(1), field_all, coef, fold_low, grad_mixed, rest)
    if fine:
        late_mine, late_other, *_ = lax.optimization_barrier((late_mine, late_other, *agg_job.send_all()))
    late_job = SumRows(late_mine, late_other)
    if fine:
        edge_job = SplitSum.joined([end_job, pair_job])
        sent = [*edge_job.send_blocks(), two_job.end(), one_job.end()]
        late_job.step()
        late_job.job.cur = after(late_job.job.cur, *sent)
        agg_job.send_blocks()
        plan = (
            [(12 + f, f, 0) for f in range(folds)],
            [(8 + f, 0, f) for f in range(folds)],
            [(m, i, 0) for i, m in enumerate((4, 7, 5, 6))],
            [(3, 0, 0)],
        )
        by_slot, square = finish(slot_of, plan, [j.parts() for j in (two_job, one_job, edge_job, agg_job)])
        part_square = jnp.sum(square)
        while len(late_job.steps) > 1:
            late_job.step()
        by_slot, late_job.cur = lax.optimization_barrier((by_slot, late_job.cur))
        by_slot = lax.all_to_all(by_slot, "dp", 0, 0, tiled=True).astype(f32)
        slot_grads = by_slot.reshape(n_dp // 2, 2, slots, rows, half).transpose(2, 0, 3, 1, 4).reshape(slots, tall, D)
    else:
        rest = [tn(mixed, grad_h0_low), tn(own1_low, grad_query), tn(normed1_low, grad_keys),
                tn(normed1_low, grad_values), tn(attended_low, grad_h1_low)]
        rest += [tn(normed2_low, grad_pre_low[:, f * D : (f + 1) * D]) for f in range(folds)]
        rest += [tn(activ_low[:, f * D : (f + 1) * D], grad_h2_low) for f in range(folds)]
        by_slot = jnp.zeros((n_tiles, D, D), f32)
        for m, grad in enumerate(rest):
            by_slot = lax.dynamic_update_index_in_dim(by_slot, grad, slot_of[m + 3], 0)
        slot_grads = lax.psum_scatter(by_slot, "dp", scatter_dimension=0, tiled=True)
        slot_grads = lax.psum_scatter(slot_grads, "blk", scatter_dimension=1, tiled=True)
        part_square = jnp.sum(slot_grads * slot_grads)
    late = late_job.end()
    numbers = sum_small(jnp.pad(jnp.stack([part_square, loss_local]), (0, 6)))
    loss = numbers[1]
    clips, grad_key, grad_agg, vectors_new, vec_m_new, vec_v_new = tail(
        numbers[:1], first, embed_hi, embed_lo, gram, fold_key, query_f, fold_vecs, late, vectors, vec_m, vec_v
    )
    clip, grad_norm = clips[0, 0], clips[0, 1]

    at_rows = blk * tall
    var_query_f = extras[0].astype(bf16).astype(f32)
    own_first = lax.dynamic_slice_in_dim(var_query_f, at_rows, tall, 0)[:, None] * grad_agg[0][None, :]
    own_key = lax.dynamic_slice_in_dim(grad_key, at_rows, tall, 1)
    own_second = jnp.repeat(own_key.T, HD, axis=1) * query_f[0][None, :]
    own_third = lax.dot_general(
        lax.dynamic_slice_in_dim(embed, at_rows, tall, 1), late[:TABLE], (((0,), (0,)), ((), ())),
        precision=HIGHEST, preferred_element_type=f32,
    )
    my_tiles = [jnp.sum(jnp.where(slot_of == dp * slots + t, jnp.arange(n_tiles), 0)) for t in range(slots)]
    shard_grads = jnp.stack(
        [
            jnp.where(m == 0, own_first, jnp.where(m == 1, own_second, jnp.where(m == 2, own_third, slot_grads[t])))
            for t, m in enumerate(my_tiles)
        ]
    )
    tiles_new, tiles_m_new, tiles_v_new = adam_update(tiles, shard_grads * clip, tiles_m, tiles_v, rate_tiles)
    return (loss, grad_norm, tiles_new, tiles_m_new, tiles_v_new, vectors_new, vec_m_new, vec_v_new)


def solution(mesh):
    tile = P("dp", "blk", None)
    placed = (tile, tile, P("dp"), tile, P("dp"), P(), tile, tile, tile, P(), P(), P())
    return jax.shard_map(
        shards,
        mesh=mesh,
        in_specs=placed,
        out_specs=(P(), P(), tile, tile, tile, P(), P(), P()),
        check_vma=False,
    )
```
